32 devices in a mesh: dp: 8 (over z, core), tensor: 4 (over y, x).
Axes of the slice: x: 2, y: 2, z: 4, core: 2. Of those that a mesh axis runs over, the one named last changes fastest.
Arguments:
- queries: bfloat16 [4096, 4096], P('dp')
- keys: bfloat16 [4096, 4096], P('dp')
- projection: bfloat16 [4096, 1024], P(None, 'tensor'), may hold values from -0.09375 to 0.09375
- positives: int32 [8, 512], P('dp'), may hold values from 0 to 511, each once within a row
Outputs:
- pair_loss: float32 [4096], P(('dp', 'tensor'))
- grad_queries: float32 [4096, 1024], P(('dp', 'tensor'))
- grad_keys: float32 [4096, 1024], P(('dp', 'tensor'))
The draws below stay inside these ranges and needn't reach their ends.
Inputs may be any that keep to these rules, and one draw needn't show every extreme that they name: Each row of positives holds every number of 0 to 511 once.
All inputs are finite; a program needn't handle non-finite values.
Results may differ from the reference program's by a relative error of at most 0.0069.
Values may be sent and summed in bfloat16 or wider, within the bound.
A program may use at most 128 MiB of HBM per device.

```python
import jax
import jax.numpy as jnp
from jax import lax

D = 4096
E = 1024
ROWS = 512
PAIRS = 4096
N_DP = 8


def draw_both(seeded):
    mixed = jax.random.fold_in(seeded, 4093)
    subkeys = jax.random.split(mixed, 2)
    query_draw = jax.random.normal(subkeys[0], (PAIRS, D), jnp.float32)
    key_draw = jax.random.normal(subkeys[1], (PAIRS, D), jnp.float32)
    return (query_draw, key_draw)


def draw_queries(key, part):
    return draw_both(key)[0].astype(jnp.bfloat16)


def draw_keys(key, part):
    return draw_both(key)[1].astype(jnp.bfloat16)


def levels(own_key, dims, shards, smallest, top_value):
    factor_of = 1.0
    for dim, shards_of in shards:
        draws = jax.random.uniform(jax.random.fold_in(jax.random.fold_in(own_key, 6), dim), (shards_of,), jnp.float32, smallest / len(shards), top_value / len(shards))
        factor_of = factor_of * jnp.repeat(jnp.exp(draws), dims[dim] // shards_of).reshape((-1,) + (1,) * (len(dims) - 1 - dim))
    return factor_of


def centred(rng, shape, width, bound, shards=(), kind=jnp.bfloat16):
    factor_of = levels(rng, shape, shards, -0.22, 0.18) if shards else 1.0
    values = jax.random.normal(rng, shape, jnp.float32) * width * factor_of
    return jnp.minimum(jnp.maximum(values, -bound), bound).astype(kind)


def setup_inputs(seed: int = 0) -> dict:
    arg_keys = jax.random.split(jax.random.key(seed), 5)
    return {
        "queries": draw_queries(jax.random.fold_in(arg_keys[4], 71), 0),
        "keys": draw_keys(jax.random.fold_in(arg_keys[4], 71), 0),
        "projection": centred(arg_keys[2], (D, E), D ** -0.5, 0.09375, ((1, 4),)),
        "positives": jax.vmap(lambda own: jax.random.permutation(own, ROWS))(jax.random.split(arg_keys[3], N_DP)).reshape((N_DP, ROWS)).astype(jnp.int32),
    }


SCALE = 100.0
EPSILON = 1e-06

def normalize(embedding):
    entries = embedding.astype(jnp.float32)
    magnitude = jnp.sqrt(lax.optimization_barrier(jnp.sum(entries * entries, axis=1, keepdims=True)) + EPSILON)
    return (entries / magnitude, magnitude)

def unnormalize(grad_unit, unit_rows, magnitude):
    return (grad_unit - unit_rows * lax.optimization_barrier(jnp.sum(unit_rows * grad_unit, axis=1, keepdims=True))) / magnitude

def reference(queries, keys, projection, positives):
    query_proj = jnp.dot(queries, projection, preferred_element_type=jnp.float32).astype(jnp.bfloat16)
    key_proj = jnp.dot(keys, projection, preferred_element_type=jnp.float32).astype(jnp.bfloat16)
    query_unit, query_mag = normalize(query_proj)
    key_unit, key_mag = normalize(key_proj)
    query_hat = query_unit.astype(jnp.bfloat16)
    key_hat = key_unit.astype(jnp.bfloat16)
    offsets = (jnp.arange(N_DP, dtype=jnp.int32) * ROWS)[:, None]
    targets = (positives.astype(jnp.int32) + offsets).reshape(N_DP, ROWS)
    blocks = query_hat.reshape(N_DP, ROWS, E)
    columns = jnp.arange(PAIRS, dtype=jnp.int32)[None, :]

    def one_block(grad_key_hat, inputs):
        query_block, target = inputs
        scores = SCALE * lax.dot_general(query_block, key_hat, (((1,), (1,)), ((), ())), preferred_element_type=jnp.float32)
        row_max = lax.optimization_barrier(jnp.max(scores, axis=1))
        log_total = row_max + jnp.log(lax.optimization_barrier(jnp.sum(jnp.exp(scores - row_max[:, None]), axis=1)))
        positive_mask = (columns == target[:, None]).astype(jnp.float32)
        matched = lax.optimization_barrier(jnp.sum(scores * positive_mask, axis=1))
        weights = (jnp.exp(scores - log_total[:, None]) - positive_mask).astype(jnp.bfloat16)
        grad_q = SCALE * jnp.dot(weights, key_hat, preferred_element_type=jnp.float32)
        grad_key_hat = grad_key_hat + SCALE * lax.dot_general(weights, query_block, (((0,), (0,)), ((), ())), preferred_element_type=jnp.float32)
        return (grad_key_hat, (log_total - matched, grad_q))
    grad_key_hat, (losses, grad_query_hat) = lax.scan(one_block, jnp.zeros((PAIRS, E), jnp.float32), (blocks, targets))
    pair_loss = losses.reshape(PAIRS)
    grad_queries = unnormalize(grad_query_hat.reshape(PAIRS, E), query_unit, query_mag)
    grad_keys = unnormalize(grad_key_hat, key_unit, key_mag)
    return (pair_loss, grad_queries, grad_keys)
```

```python
import functools

import jax
import jax.numpy as jnp
from jax import lax
from jax.experimental import pallas as pl
from jax.experimental.pallas import tpu as pltpu
from jax.sharding import PartitionSpec as P

SCALE = 100.0
EPSILON = 1e-06
MESH = pl.DeviceIdType.MESH
HALVES = 2


def kernel(
    chips, groups, q_ref, k_ref, pos_ref, loss_ref, gq_ref, gk_ref,
    kraw, kunit, kall, qraw, qhat, scores, weights, stats,
    sib_out, sib_in, ring_out, ring_in, gq_out, gq_in,
    kx_send, kx_recv, qx_send, qx_recv, ring_send, fwd_send, k_recv,
    st_send, st_recv, sb_send, sb_recv, rg_send, rg_recv, gq_send, gq_recv,
):
    rows, feats = q_ref.shape
    part = rows // groups
    half = part // HALVES
    me = lax.axis_index("dp")
    t = lax.axis_index("tensor")
    chip, core = me // 2, me % 2
    other = 1 - core
    sibling = chip * 2 + other
    right = lax.rem(chip + 1, chips) * 2 + core
    left = lax.rem(chip + chips - 1, chips) * 2 + core

    def peer(i):
        return lax.rem(t + i, groups)

    def remote(src, dst, send, recv, device):
        return pltpu.make_async_remote_copy(
            src_ref=src, dst_ref=dst, send_sem=send, recv_sem=recv,
            device_id=device, device_id_type=MESH,
        )

    barrier = pltpu.get_barrier_semaphore()
    for i in range(1, groups):
        pl.semaphore_signal(barrier, inc=1, device_id=(me, peer(i)), device_id_type=MESH)
    for device in (sibling, right, left):
        pl.semaphore_signal(barrier, inc=1, device_id=(device, t), device_id_type=MESH)
    pl.semaphore_wait(barrier, groups + 2)

    def kx_copy(i):
        rows_of = pl.ds(pl.multiple_of(peer(i) * part, part), part)
        return remote(k_ref.at[rows_of], kraw.at[t], kx_send.at[i], kx_recv.at[t], (me, peer(i)))

    def kx_from(i):
        slot = kraw.at[peer(i)]
        return remote(slot, slot, kx_send.at[i], kx_recv.at[peer(i)], (me, peer(i)))

    def qx_copy(i):
        return remote(q_ref, qraw.at[t], qx_send.at[i], qx_recv.at[t], (me, peer(i)))

    def qx_from(i):
        slot = qraw.at[peer(i)]
        return remote(slot, slot, qx_send.at[i], qx_recv.at[peer(i)], (me, peer(i)))

    for i in range(1, groups):
        kx_copy(i).start()
    kraw[t] = k_ref[pl.ds(pl.multiple_of(t * part, part), part)]
    qraw[t] = q_ref[...]
    for i in range(1, groups):
        kx_from(i).wait_recv()

    def inverse_magnitude(blocks):
        total = blocks[0] * blocks[0]
        for block in blocks[1:]:
            total = total + block * block
        return lax.rsqrt(jnp.sum(total, axis=1, keepdims=True) + EPSILON)

    entries = [kraw[s].astype(jnp.float32) for s in range(groups)]
    k_inverse = inverse_magnitude(entries)
    for s in range(groups):
        unit = entries[s] * k_inverse
        kunit[:, s * feats : (s + 1) * feats] = unit
        kall[me, :, s * feats : (s + 1) * feats] = unit.astype(jnp.bfloat16)

    def source(s):
        return lax.rem(chip + chips - s, chips) * 2

    def ring_copy(s, h):
        slot = kall.at[source(s) + core, pl.ds(h * half, half)]
        return remote(slot, slot, ring_send.at[s, h], k_recv.at[source(s) + core, h], (right, t))

    def fwd_copy(s, h):
        slot = kall.at[source(s) + core, pl.ds(h * half, half)]
        return remote(slot, slot, fwd_send.at[s, h], k_recv.at[source(s) + core, h], (sibling, t))

    def k_from(index, h):
        slot = kall.at[index, pl.ds(h * half, half)]
        return remote(slot, slot, ring_send.at[0, h], k_recv.at[index, h], (right, t))

    def forward(s):
        for h in range(HALVES):
            if s > 0:
                k_from(source(s) + core, h).wait_recv()
            if s < chips - 1:
                ring_copy(s, h).start()
            fwd_copy(s, h).start()

    forward(0)
    for i in range(1, groups):
        qx_copy(i).start()
    for s in range(1, chips - 1):
        forward(s)

    for i in range(1, groups):
        qx_from(i).wait_recv()

    def normalize_rows(p, carried):
        span = pl.ds(pl.multiple_of(p * part, part), part)
        blocks = [qraw[s, span].astype(jnp.float32) for s in range(groups)]
        inverse = inverse_magnitude(blocks)
        for s in range(groups):
            qhat[span, s * feats : (s + 1) * feats] = (blocks[s] * inverse).astype(jnp.bfloat16)
        return carried

    lax.fori_loop(0, groups, normalize_rows, 0)

    def score(index):
        block = SCALE * lax.dot_general(
            kall[index], qhat[...], (((1,), (1,)), ((), ())), preferred_element_type=jnp.float32
        )
        scores[index] = block
        return block

    def fold(index, state):
        row_max, row_sum = state
        block = score(index)
        new_max = jnp.maximum(row_max, jnp.max(block, axis=0, keepdims=True))
        row_sum = row_sum * jnp.exp(row_max - new_max) + jnp.sum(
            jnp.exp(block - new_max), axis=0, keepdims=True
        )
        return (new_max, row_sum)

    def positive_mask():
        key_index = lax.broadcasted_iota(jnp.int32, (part, rows), 0)
        return (key_index == pos_ref[...] - t * part).astype(jnp.float32)

    own = score(me)
    row_max = jnp.max(own, axis=0, keepdims=True)
    row_sum = jnp.sum(jnp.exp(own - row_max), axis=0, keepdims=True)
    matched = jnp.sum(own * positive_mask(), axis=0, keepdims=True)

    def from_sibling(s):
        for h in range(HALVES):
            k_from(source(s) + other, h).wait_recv()

    def fold_pair(s, state):
        state = fold(source(s) + core, state)
        from_sibling(s)
        return fold(source(s) + other, state)

    from_sibling(0)
    state = fold(source(0) + other, (row_max, row_sum))
    state = lax.fori_loop(1, chips - 1, fold_pair, state)
    forward(chips - 1)
    row_max, row_sum = fold_pair(chips - 1, state)

    stats[t, 0:1] = row_max
    stats[t, 1:2] = row_sum
    stats[t, 2:3] = matched

    def st_copy(i):
        return remote(stats.at[t], stats.at[t], st_send.at[i], st_recv.at[t], (me, peer(i)))

    def st_from(i):
        slot = stats.at[peer(i)]
        return remote(slot, slot, st_send.at[i], st_recv.at[peer(i)], (me, peer(i)))

    for i in range(1, groups):
        st_copy(i).start()
    for i in range(1, groups):
        st_from(i).wait_recv()
    best = stats[0, 0:1]
    for s in range(1, groups):
        best = jnp.maximum(best, stats[s, 0:1])
    total = jnp.zeros_like(best)
    matched = jnp.zeros_like(best)
    for s in range(groups):
        total = total + stats[s, 1:2] * jnp.exp(stats[s, 0:1] - best)
        matched = matched + stats[s, 2:3]
    log_total = best + jnp.log(total)
    loss_ref[...] = log_total - matched

    def weigh(index, carried):
        weights[index] = jnp.exp(scores[index] - log_total).astype(jnp.bfloat16)
        return carried

    lax.fori_loop(0, 2 * chips, weigh, 0)
    weights[me] = (jnp.exp(scores[me] - log_total) - positive_mask()).astype(jnp.bfloat16)

    def target(i):
        return lax.rem(chip + 2 * chips - 1 - i, chips) * 2

    def key_part(index):
        return jnp.dot(weights[index], qhat[...], preferred_element_type=jnp.float32)

    def sb_copy(i):
        return remote(sib_out.at[i], sib_in.at[i], sb_send.at[i], sb_recv.at[i], (sibling, t))

    def rg_copy(i, h):
        span = pl.ds(h * half, half)
        return remote(
            ring_out.at[i, span], ring_in.at[i, span], rg_send.at[i, h], rg_recv.at[i, h], (right, t)
        )

    def hand_over(i, carried):
        sib_out[i] = key_part(target(i) + other).astype(jnp.bfloat16)
        sb_copy(i).start()
        return carried

    def ring_first():
        value = key_part(target(0) + core)
        sb_copy(0).wait_recv()
        for h in range(HALVES):
            span = slice(h * half, (h + 1) * half)
            ring_out[0, span] = (value[span] + sib_in[0, span].astype(jnp.float32)).astype(jnp.bfloat16)
            rg_copy(0, h).start()

    def ring_next(i, carried):
        value = key_part(target(i) + core)
        sb_copy(i).wait_recv()
        for h in range(HALVES):
            span = slice(h * half, (h + 1) * half)
            both = value[span] + sib_in[i, span].astype(jnp.float32)
            rg_copy(i - 1, h).wait_recv()
            ring_out[i, span] = (both + ring_in[i - 1, span].astype(jnp.float32)).astype(jnp.bfloat16)
            rg_copy(i, h).start()
        return carried

    hand_over(0, 0)
    ring_first()
    lax.fori_loop(1, chips, hand_over, 0)

    def query_part(p):
        span = pl.ds(pl.multiple_of(p * part, part), part)
        chosen = weights[:, :, span].reshape(2 * chips * part, part)
        keys = kall[...].reshape(2 * chips * part, groups * feats)
        return lax.dot_general(
            chosen, keys, (((0,), (0,)), ((), ())), preferred_element_type=jnp.float32
        )

    def gq_copy(i):
        return remote(gq_out.at[i - 1], gq_in.at[i - 1], gq_send.at[i - 1], gq_recv.at[i - 1], (me, peer(i)))

    def query_send(i, carried):
        gq_out[i - 1] = query_part(peer(i)).astype(jnp.bfloat16)
        gq_copy(i).start()
        return carried

    lax.fori_loop(1, groups, query_send, 0)
    gq_ref[...] = query_part(t)
    lax.fori_loop(1, chips - 1, ring_next, 0)

    def unnormalized(grad, unit, inverse):
        grad = grad * SCALE
        return (grad - unit * jnp.sum(unit * grad, axis=1, keepdims=True)) * inverse

    value = gq_ref[...]
    for i in range(1, groups):
        gq_copy(i).wait_recv()
        value = value + gq_in[i - 1].astype(jnp.float32)
    own_rows = pl.ds(pl.multiple_of(t * part, part), part)
    blocks = [qraw[s, own_rows].astype(jnp.float32) for s in range(groups)]
    inverse = inverse_magnitude(blocks)
    gq_ref[...] = unnormalized(value, jnp.concatenate(blocks, axis=1) * inverse, inverse)

    value = key_part(me)
    sb_copy(chips - 1).wait_recv()
    value = value + sib_in[chips - 1].astype(jnp.float32)
    for h in range(HALVES):
        rg_copy(chips - 2, h).wait_recv()
    value = value + ring_in[chips - 2].astype(jnp.float32)
    gk_ref[...] = unnormalized(value, kunit[...], k_inverse)

    for i in range(1, groups):
        kx_copy(i).wait_send()
        qx_copy(i).wait_send()
        st_copy(i).wait_send()
        gq_copy(i).wait_send()
    for s in range(chips):
        sb_copy(s).wait_send()
        for h in range(HALVES):
            fwd_copy(s, h).wait_send()
            if s < chips - 1:
                ring_copy(s, h).wait_send()
                rg_copy(s, h).wait_send()


def body(queries, keys, projection, positives):
    dp, groups = lax.axis_size("dp"), lax.axis_size("tensor")
    chips = dp // 2
    rows = queries.shape[0]
    part = rows // groups
    feats = projection.shape[1]
    width = feats * groups
    key_feats = jnp.dot(keys, projection, preferred_element_type=jnp.float32).astype(jnp.bfloat16)
    query_feats = jnp.dot(queries, projection, preferred_element_type=jnp.float32).astype(jnp.bfloat16)
    bf16, f32 = jnp.bfloat16, jnp.float32
    vmem, dma = pltpu.VMEM, pltpu.SemaphoreType.DMA
    spec = pl.BlockSpec(memory_space=pltpu.VMEM)
    loss, grad_q, grad_k = pl.pallas_call(
        functools.partial(kernel, chips, groups),
        out_shape=(
            jax.ShapeDtypeStruct((1, rows), f32),
            jax.ShapeDtypeStruct((part, width), f32),
            jax.ShapeDtypeStruct((part, width), f32),
        ),
        in_specs=[spec] * 3,
        out_specs=(spec,) * 3,
        scratch_shapes=[
            vmem((groups, part, feats), bf16),
            vmem((part, width), f32),
            vmem((dp, part, width), bf16),
            vmem((groups, rows, feats), bf16),
            vmem((rows, width), bf16),
            vmem((dp, part, rows), f32),
            vmem((dp, part, rows), bf16),
            vmem((groups, 8, rows), f32),
            vmem((chips, part, width), bf16),
            vmem((chips, part, width), bf16),
            vmem((chips - 1, part, width), bf16),
            vmem((chips - 1, part, width), bf16),
            vmem((groups - 1, part, width), bf16),
            vmem((groups - 1, part, width), bf16),
            dma((groups,)), dma((groups,)), dma((groups,)), dma((groups,)),
            dma((chips, HALVES)), dma((chips, HALVES)), dma((dp, HALVES)),
            dma((groups,)), dma((groups,)),
            dma((chips,)), dma((chips,)),
            dma((chips, HALVES)), dma((chips, HALVES)),
            dma((groups,)), dma((groups,)),
        ],
        compiler_params=pltpu.CompilerParams(
            collective_id=0, has_side_effects=True, vmem_limit_bytes=60 * 1024 * 1024
        ),
        cost_estimate=pl.CostEstimate(
            flops=8 * rows * dp * part * width, bytes_accessed=8 * part * width * 4,
            transcendentals=2 * rows * dp * part,
        ),
    )(query_feats, key_feats, positives)
    row_start = lax.axis_index("tensor") * part
    pair_loss = lax.dynamic_slice_in_dim(loss[0], row_start, part, 0)
    return (pair_loss, grad_q, grad_k)


def solution(mesh):
    in_specs = (P("dp", None), P("dp", None), P(None, "tensor"), P("dp", None))
    out_specs = (P(("dp", "tensor")), P(("dp", "tensor"), None), P(("dp", "tensor"), None))
    return jax.shard_map(body, mesh=mesh, in_specs=in_specs, out_specs=out_specs, check_vma=False)
```

```python
import functools

import jax
import jax.numpy as jnp
from jax import lax
from jax.experimental import pallas as pl
from jax.experimental.pallas import tpu as pltpu
from jax.sharding import PartitionSpec as P

SCALE = 100.0
EPSILON = 1e-06
MESH = pl.DeviceIdType.MESH
HALVES = 2
DEPTH = 512
STAGE_BYTES = 4 * 1024 * 1024


def kernel(
    chips, groups, q_hbm, k_hbm, w_hbm, pos_ref, loss_ref, gq_ref, gk_ref,
    stage, w_in, kfeat, kraw, kall, qraw, qhat, scores, weights, stats,
    sib_out, sib_in, ring_in, gq_out, gq_in, stage_sem, w_sem,
    kx_send, kx_recv, qx_send, qx_recv, ring_send, fwd_send, k_recv,
    st_send, st_recv, sb_send, sb_recv, rg_send, rg_recv, gq_send, gq_recv,
):
    rows, feats = kfeat.shape
    slots, steps = stage.shape[0], w_in.shape[0] // DEPTH
    part = rows // groups
    half = part // HALVES
    me = lax.axis_index("dp")
    t = lax.axis_index("tensor")
    chip, core = me // 2, me % 2
    other = 1 - core
    sibling = chip * 2 + other
    right = lax.rem(chip + 1, chips) * 2 + core
    left = lax.rem(chip + chips - 1, chips) * 2 + core

    def peer(i):
        return lax.rem(t + i, groups)

    def remote(src, dst, send, recv, device):
        return pltpu.make_async_remote_copy(
            src_ref=src, dst_ref=dst, send_sem=send, recv_sem=recv,
            device_id=device, device_id_type=MESH,
        )

    barrier = pltpu.get_barrier_semaphore()
    for i in range(1, groups):
        pl.semaphore_signal(barrier, inc=1, device_id=(me, peer(i)), device_id_type=MESH)
    for device in (sibling, right, left):
        pl.semaphore_signal(barrier, inc=1, device_id=(device, t), device_id_type=MESH)

    def w_copy(c):
        span = pl.ds(c * DEPTH, DEPTH)
        return pltpu.make_async_copy(w_hbm.at[span], w_in.at[span], w_sem.at[c])

    def stage_copy(c):
        source_ref = k_hbm if c < steps else q_hbm
        span = pl.ds((c % steps) * DEPTH, DEPTH)
        return pltpu.make_async_copy(
            source_ref.at[:, span], stage.at[c % slots], stage_sem.at[c % slots]
        )

    for c in range(max(steps, slots)):
        if c < steps:
            w_copy(c).start()
        if c < slots:
            stage_copy(c).start()

    def project(first):
        total = None
        for c in range(steps):
            if first == 0:
                w_copy(c).wait()
            stage_copy(first + c).wait()
            term = jnp.dot(
                stage[(first + c) % slots], w_in[c * DEPTH : (c + 1) * DEPTH],
                preferred_element_type=jnp.float32,
            )
            total = term if total is None else total + term
            if first + c + slots < 2 * steps:
                stage_copy(first + c + slots).start()
        return total.astype(jnp.bfloat16)

    kfeat[...] = project(0)
    pl.semaphore_wait(barrier, groups + 2)

    def kx_copy(i):
        rows_of = pl.ds(pl.multiple_of(peer(i) * part, part), part)
        return remote(kfeat.at[rows_of], kraw.at[t], kx_send.at[i], kx_recv.at[t], (me, peer(i)))

    def kx_from(i):
        slot = kraw.at[peer(i)]
        return remote(slot, slot, kx_send.at[i], kx_recv.at[peer(i)], (me, peer(i)))

    def qx_copy(i):
        return remote(qraw.at[t], qraw.at[t], qx_send.at[i], qx_recv.at[t], (me, peer(i)))

    def qx_from(i):
        slot = qraw.at[peer(i)]
        return remote(slot, slot, qx_send.at[i], qx_recv.at[peer(i)], (me, peer(i)))

    for i in range(1, groups):
        kx_copy(i).start()
    kraw[t] = kfeat[pl.ds(pl.multiple_of(t * part, part), part)]
    qraw[t] = project(steps)
    for i in range(1, groups):
        kx_from(i).wait_recv()

    def inverse_magnitude(blocks):
        total = blocks[0] * blocks[0]
        for block in blocks[1:]:
            total = total + block * block
        return lax.rsqrt(jnp.sum(total, axis=1, keepdims=True) + EPSILON)

    entries = [kraw[s].astype(jnp.float32) for s in range(groups)]
    k_inverse = inverse_magnitude(entries)
    for s in range(groups):
        kall[me, :, s * feats : (s + 1) * feats] = (entries[s] * k_inverse).astype(
            jnp.bfloat16
        )

    def source(s):
        return lax.rem(chip + chips - s, chips) * 2

    def ring_copy(s, h):
        slot = kall.at[source(s) + core, pl.ds(h * half, half)]
        return remote(slot, slot, ring_send.at[s, h], k_recv.at[source(s) + core, h], (right, t))

    def fwd_copy(s, h):
        slot = kall.at[source(s) + core, pl.ds(h * half, half)]
        return remote(slot, slot, fwd_send.at[s, h], k_recv.at[source(s) + core, h], (sibling, t))

    def k_from(index, h):
        slot = kall.at[index, pl.ds(h * half, half)]
        return remote(slot, slot, ring_send.at[0, h], k_recv.at[index, h], (right, t))

    def forward(s):
        for h in range(HALVES):
            if s > 0:
                k_from(source(s) + core, h).wait_recv()
            if s < chips - 1:
                ring_copy(s, h).start()
            fwd_copy(s, h).start()

    forward(0)
    for i in range(1, groups):
        qx_copy(i).start()
    for s in range(1, chips - 1):
        forward(s)

    for i in range(1, groups):
        qx_from(i).wait_recv()

    def normalize_rows(p, carried):
        span = pl.ds(pl.multiple_of(p * part, part), part)
        blocks = [qraw[s, span].astype(jnp.float32) for s in range(groups)]
        inverse = inverse_magnitude(blocks)
        for s in range(groups):
            qhat[span, s * feats : (s + 1) * feats] = (blocks[s] * inverse).astype(jnp.bfloat16)
        return carried

    lax.fori_loop(0, groups, normalize_rows, 0)

    def score(index):
        block = SCALE * lax.dot_general(
            kall[index], qhat[...], (((1,), (1,)), ((), ())), preferred_element_type=jnp.float32
        )
        scores[index] = block
        return block

    def fold(index, state):
        row_max, row_sum = state
        block = score(index)
        new_max = jnp.maximum(row_max, jnp.max(block, axis=0, keepdims=True))
        row_sum = row_sum * jnp.exp(row_max - new_max) + jnp.sum(
            jnp.exp(block - new_max), axis=0, keepdims=True
        )
        return (new_max, row_sum)

    def positive_mask():
        key_index = lax.broadcasted_iota(jnp.int32, (part, rows), 0)
        return (key_index == pos_ref[...] - t * part).astype(jnp.float32)

    own = score(me)
    row_max = jnp.max(own, axis=0, keepdims=True)
    row_sum = jnp.sum(jnp.exp(own - row_max), axis=0, keepdims=True)
    matched = jnp.sum(own * positive_mask(), axis=0, keepdims=True)

    def from_sibling(s):
        for h in range(HALVES):
            k_from(source(s) + other, h).wait_recv()

    def fold_pair(s, state):
        state = fold(source(s) + core, state)
        from_sibling(s)
        return fold(source(s) + other, state)

    from_sibling(0)
    state = fold(source(0) + other, (row_max, row_sum))
    state = lax.fori_loop(1, chips - 1, fold_pair, state)
    forward(chips - 1)
    row_max, row_sum = fold_pair(chips - 1, state)

    stats[t, 0:1] = row_max
    stats[t, 1:2] = row_sum
    stats[t, 2:3] = matched

    def st_copy(i):
        return remote(stats.at[t], stats.at[t], st_send.at[i], st_recv.at[t], (me, peer(i)))

    def st_from(i):
        slot = stats.at[peer(i)]
        return remote(slot, slot, st_send.at[i], st_recv.at[peer(i)], (me, peer(i)))

    for i in range(1, groups):
        st_copy(i).start()
    for i in range(1, groups):
        st_from(i).wait_recv()
    best = stats[0, 0:1]
    for s in range(1, groups):
        best = jnp.maximum(best, stats[s, 0:1])
    total = jnp.zeros_like(best)
    matched = jnp.zeros_like(best)
    for s in range(groups):
        total = total + stats[s, 1:2] * jnp.exp(stats[s, 0:1] - best)
        matched = matched + stats[s, 2:3]
    log_total = best + jnp.log(total)
    loss_ref[...] = log_total - matched

    def weigh(index, carried):
        weights[index] = jnp.exp(scores[index] - log_total).astype(jnp.bfloat16)
        return carried

    lax.fori_loop(0, 2 * chips, weigh, 0)
    weights[me] = (jnp.exp(scores[me] - log_total) - positive_mask()).astype(jnp.bfloat16)

    def target(i):
        return lax.rem(chip + 2 * chips - 1 - i, chips) * 2

    def key_part(index):
        return jnp.dot(weights[index], qhat[...], preferred_element_type=jnp.float32)

    def sb_copy(i):
        return remote(sib_out.at[i], sib_in.at[i], sb_send.at[i], sb_recv.at[i], (sibling, t))

    def rg_copy(i, h):
        span = pl.ds(h * half, half)
        return remote(
            sib_in.at[i, span], ring_in.at[i, span], rg_send.at[i, h], rg_recv.at[i, h], (right, t)
        )

    def hand_over(i, carried):
        sib_out[i] = key_part(target(i) + other).astype(jnp.bfloat16)
        sb_copy(i).start()
        return carried

    def ring_first():
        value = key_part(target(0) + core)
        sb_copy(0).wait_recv()
        for h in range(HALVES):
            span = slice(h * half, (h + 1) * half)
            sib_in[0, span] = (value[span] + sib_in[0, span].astype(jnp.float32)).astype(jnp.bfloat16)
            rg_copy(0, h).start()

    def ring_next(i, carried):
        value = key_part(target(i) + core)
        sb_copy(i).wait_recv()
        for h in range(HALVES):
            span = slice(h * half, (h + 1) * half)
            both = value[span] + sib_in[i, span].astype(jnp.float32)
            rg_copy(i - 1, h).wait_recv()
            sib_in[i, span] = (both + ring_in[i - 1, span].astype(jnp.float32)).astype(jnp.bfloat16)
            rg_copy(i, h).start()
        return carried

    hand_over(0, 0)
    ring_first()
    lax.fori_loop(1, chips, hand_over, 0)

    def query_part(p):
        span = pl.ds(pl.multiple_of(p * part, part), part)
        chosen = weights[:, :, span].reshape(2 * chips * part, part)
        keys = kall[...].reshape(2 * chips * part, groups * feats)
        return lax.dot_general(
            chosen, keys, (((0,), (0,)), ((), ())), preferred_element_type=jnp.float32
        )

    def gq_copy(i):
        return remote(gq_out.at[i - 1], gq_in.at[i - 1], gq_send.at[i - 1], gq_recv.at[i - 1], (me, peer(i)))

    def query_send(i, carried):
        gq_out[i - 1] = query_part(peer(i)).astype(jnp.bfloat16)
        gq_copy(i).start()
        return carried

    lax.fori_loop(1, groups, query_send, 0)
    gq_ref[...] = query_part(t)
    lax.fori_loop(1, chips - 1, ring_next, 0)

    def unnormalized(grad, unit, inverse):
        grad = grad * SCALE
        return (grad - unit * jnp.sum(unit * grad, axis=1, keepdims=True)) * inverse

    value = gq_ref[...]
    for i in range(1, groups):
        gq_copy(i).wait_recv()
        value = value + gq_in[i - 1].astype(jnp.float32)
    own_rows = pl.ds(pl.multiple_of(t * part, part), part)
    blocks = [qraw[s, own_rows].astype(jnp.float32) for s in range(groups)]
    inverse = inverse_magnitude(blocks)
    gq_ref[...] = unnormalized(value, jnp.concatenate(blocks, axis=1) * inverse, inverse)

    value = key_part(me)
    sb_copy(chips - 1).wait_recv()
    value = value + sib_in[chips - 1].astype(jnp.float32)
    for h in range(HALVES):
        rg_copy(chips - 2, h).wait_recv()
    value = value + ring_in[chips - 2].astype(jnp.float32)
    blocks = [kraw[s].astype(jnp.float32) for s in range(groups)]
    inverse = inverse_magnitude(blocks)
    gk_ref[...] = unnormalized(value, jnp.concatenate(blocks, axis=1) * inverse, inverse)

    for i in range(1, groups):
        kx_copy(i).wait_send()
        qx_copy(i).wait_send()
        st_copy(i).wait_send()
        gq_copy(i).wait_send()
    for s in range(chips):
        sb_copy(s).wait_send()
        for h in range(HALVES):
            fwd_copy(s, h).wait_send()
            if s < chips - 1:
                ring_copy(s, h).wait_send()
                rg_copy(s, h).wait_send()


def body(queries, keys, projection, positives):
    dp, groups = lax.axis_size("dp"), lax.axis_size("tensor")
    chips = dp // 2
    rows = queries.shape[0]
    part = rows // groups
    feats = projection.shape[1]
    width = feats * groups
    embed = queries.shape[1]
    slots = min(STAGE_BYTES // (rows * DEPTH * 2), embed // DEPTH)
    bf16, f32 = jnp.bfloat16, jnp.float32
    vmem, dma = pltpu.VMEM, pltpu.SemaphoreType.DMA
    spec = pl.BlockSpec(memory_space=pltpu.VMEM)
    loss, grad_q, grad_k = pl.pallas_call(
        functools.partial(kernel, chips, groups),
        out_shape=(
            jax.ShapeDtypeStruct((1, rows), f32),
            jax.ShapeDtypeStruct((part, width), f32),
            jax.ShapeDtypeStruct((part, width), f32),
        ),
        in_specs=[pl.BlockSpec(memory_space=pl.ANY)] * 3 + [spec],
        out_specs=(spec,) * 3,
        scratch_shapes=[
            vmem((slots, rows, DEPTH), bf16),
            vmem((embed, feats), bf16),
            vmem((rows, feats), bf16),
            vmem((groups, part, feats), bf16),
            vmem((dp, part, width), bf16),
            vmem((groups, rows, feats), bf16),
            vmem((rows, width), bf16),
            vmem((dp, part, rows), f32),
            vmem((dp, part, rows), bf16),
            vmem((groups, 8, rows), f32),
            vmem((chips, part, width), bf16),
            vmem((chips, part, width), bf16),
            vmem((chips - 1, part, width), bf16),
            vmem((groups - 1, part, width), bf16),
            vmem((groups - 1, part, width), bf16),
            dma((slots,)), dma((embed // DEPTH,)),
            dma((groups,)), dma((groups,)), dma((groups,)), dma((groups,)),
            dma((chips, HALVES)), dma((chips, HALVES)), dma((dp, HALVES)),
            dma((groups,)), dma((groups,)),
            dma((chips,)), dma((chips,)),
            dma((chips, HALVES)), dma((chips, HALVES)),
            dma((groups,)), dma((groups,)),
        ],
        compiler_params=pltpu.CompilerParams(
            collective_id=0, has_side_effects=True, vmem_limit_bytes=62 * 1024 * 1024
        ),
        cost_estimate=pl.CostEstimate(
            flops=8 * rows * dp * part * width + 4 * rows * embed * feats,
            bytes_accessed=(4 * rows + 2 * feats) * embed + 8 * part * width,
            transcendentals=2 * rows * dp * part,
        ),
    )(queries, keys, projection, positives)
    row_start = lax.axis_index("tensor") * part
    pair_loss = lax.dynamic_slice_in_dim(loss[0], row_start, part, 0)
    return (pair_loss, grad_q, grad_k)


def solution(mesh):
    in_specs = (P("dp", None), P("dp", None), P(None, "tensor"), P("dp", None))
    out_specs = (P(("dp", "tensor")), P(("dp", "tensor"), None), P(("dp", "tensor"), None))
    return jax.shard_map(body, mesh=mesh, in_specs=in_specs, out_specs=out_specs, check_vma=False)
```

```python
import functools

import jax
import jax.numpy as jnp
from jax import lax
from jax.experimental import pallas as pl
from jax.experimental.pallas import tpu as pltpu
from jax.sharding import PartitionSpec as P

SCALE = 100.0
EPSILON = 1e-06
MESH = pl.DeviceIdType.MESH
HALVES = 2
DEPTH = 512
STAGE_BYTES = 4 * 1024 * 1024


def kernel(
    chips, groups, q_hbm, k_hbm, w_hbm, pos_ref, loss_ref, gq_ref, gk_ref,
    stage, w_in, kfeat, kraw, kall, qraw, qhat, scores, weights, stats,
    sib_out, sib_in, ring_in, gq_out, gq_in, stage_sem, w_sem,
    kx_send, kx_recv, qx_send, qx_recv, ring_send, fwd_send, k_recv,
    st_send, st_recv, sb_send, sb_recv, rg_send, rg_recv, gq_send, gq_recv,
):
    rows, feats = kfeat.shape
    slots, steps = stage.shape[0], w_in.shape[0] // DEPTH
    part = rows // groups
    half = part // HALVES
    me = lax.axis_index("dp")
    t = lax.axis_index("tensor")
    chip, core = me // 2, me % 2
    other = 1 - core
    sibling = chip * 2 + other
    right = lax.rem(chip + 1, chips) * 2 + core
    left = lax.rem(chip + chips - 1, chips) * 2 + core

    def peer(i):
        return lax.rem(t + i, groups)

    def remote(src, dst, send, recv, device):
        return pltpu.make_async_remote_copy(
            src_ref=src, dst_ref=dst, send_sem=send, recv_sem=recv,
            device_id=device, device_id_type=MESH,
        )

    barrier = pltpu.get_barrier_semaphore()
    for i in range(1, groups):
        pl.semaphore_signal(barrier, inc=1, device_id=(me, peer(i)), device_id_type=MESH)
    for device in (sibling, right, left):
        pl.semaphore_signal(barrier, inc=1, device_id=(device, t), device_id_type=MESH)

    def w_copy(c):
        span = pl.ds(c * DEPTH, DEPTH)
        return pltpu.make_async_copy(w_hbm.at[span], w_in.at[span], w_sem.at[c])

    def stage_copy(c):
        source_ref = k_hbm if c < steps else q_hbm
        span = pl.ds((c % steps) * DEPTH, DEPTH)
        return pltpu.make_async_copy(
            source_ref.at[:, span], stage.at[c % slots], stage_sem.at[c % slots]
        )

    for c in range(max(steps, slots)):
        if c < steps:
            w_copy(c).start()
        if c < slots:
            stage_copy(c).start()

    def project(first):
        total = None
        for c in range(steps):
            if first == 0:
                w_copy(c).wait()
            stage_copy(first + c).wait()
            term = jnp.dot(
                stage[(first + c) % slots], w_in[c * DEPTH : (c + 1) * DEPTH],
                preferred_element_type=jnp.float32,
            )
            total = term if total is None else total + term
            if first + c + slots < 2 * steps:
                stage_copy(first + c + slots).start()
        return total.astype(jnp.bfloat16)

    kfeat[...] = project(0)
    pl.semaphore_wait(barrier, groups + 2)

    def kx_copy(i):
        rows_of = pl.ds(pl.multiple_of(peer(i) * part, part), part)
        return remote(kfeat.at[rows_of], kraw.at[t], kx_send.at[i], kx_recv.at[t], (me, peer(i)))

    def kx_from(i):
        slot = kraw.at[peer(i)]
        return remote(slot, slot, kx_send.at[i], kx_recv.at[peer(i)], (me, peer(i)))

    def qx_copy(i):
        return remote(qraw.at[t], qraw.at[t], qx_send.at[i], qx_recv.at[t], (me, peer(i)))

    def qx_from(i):
        slot = qraw.at[peer(i)]
        return remote(slot, slot, qx_send.at[i], qx_recv.at[peer(i)], (me, peer(i)))

    for i in range(1, groups):
        kx_copy(i).start()
    kraw[t] = kfeat[pl.ds(pl.multiple_of(t * part, part), part)]
    qraw[t] = project(steps)
    for i in range(1, groups):
        kx_from(i).wait_recv()

    def inverse_magnitude(blocks):
        total = blocks[0] * blocks[0]
        for block in blocks[1:]:
            total = total + block * block
        return lax.rsqrt(jnp.sum(total, axis=1, keepdims=True) + EPSILON)

    entries = [kraw[s].astype(jnp.float32) for s in range(groups)]
    k_inverse = inverse_magnitude(entries)
    for s in range(groups):
        kall[me, :, s * feats : (s + 1) * feats] = (entries[s] * k_inverse).astype(
            jnp.bfloat16
        )

    def source(s):
        return lax.rem(chip + chips - s, chips) * 2

    def ring_copy(s, h):
        slot = kall.at[source(s) + core, pl.ds(h * half, half)]
        return remote(slot, slot, ring_send.at[s, h], k_recv.at[source(s) + core, h], (right, t))

    def fwd_copy(s, h):
        slot = kall.at[source(s) + core, pl.ds(h * half, half)]
        return remote(slot, slot, fwd_send.at[s, h], k_recv.at[source(s) + core, h], (sibling, t))

    def k_from(index, h):
        slot = kall.at[index, pl.ds(h * half, half)]
        return remote(slot, slot, ring_send.at[0, h], k_recv.at[index, h], (right, t))

    def forward(s):
        for h in range(HALVES):
            if s > 0:
                k_from(source(s) + core, h).wait_recv()
            if s < chips - 1:
                ring_copy(s, h).start()
            fwd_copy(s, h).start()

    forward(0)
    for i in range(1, groups):
        qx_copy(i).start()
    for s in range(1, chips - 1):
        forward(s)

    for i in range(1, groups):
        qx_from(i).wait_recv()

    def normalize_rows(p, carried):
        span = pl.ds(pl.multiple_of(p * part, part), part)
        blocks = [qraw[s, span].astype(jnp.float32) for s in range(groups)]
        inverse = inverse_magnitude(blocks)
        for s in range(groups):
            qhat[span, s * feats : (s + 1) * feats] = (blocks[s] * inverse).astype(jnp.bfloat16)
        return carried

    lax.fori_loop(0, groups, normalize_rows, 0)

    def score(index):
        block = SCALE * lax.dot_general(
            kall[index], qhat[...], (((1,), (1,)), ((), ())), preferred_element_type=jnp.float32
        )
        scores[index] = block
        return block

    def fold(index, state):
        row_max, row_sum = state
        block = score(index)
        new_max = jnp.maximum(row_max, jnp.max(block, axis=0, keepdims=True))
        row_sum = row_sum * jnp.exp(row_max - new_max) + jnp.sum(
            jnp.exp(block - new_max), axis=0, keepdims=True
        )
        return (new_max, row_sum)

    def positive_mask():
        key_index = lax.broadcasted_iota(jnp.int32, (part, rows), 0)
        return (key_index == pos_ref[...] - t * part).astype(jnp.float32)

    own = score(me)
    row_max = jnp.max(own, axis=0, keepdims=True)
    row_sum = jnp.sum(jnp.exp(own - row_max), axis=0, keepdims=True)
    matched = jnp.sum(own * positive_mask(), axis=0, keepdims=True)

    def from_sibling(s):
        for h in range(HALVES):
            k_from(source(s) + other, h).wait_recv()

    def fold_pair(s, state):
        state = fold(source(s) + core, state)
        from_sibling(s)
        return fold(source(s) + other, state)

    from_sibling(0)
    state = fold(source(0) + other, (row_max, row_sum))
    state = lax.fori_loop(1, chips - 1, fold_pair, state)
    forward(chips - 1)
    row_max, row_sum = fold_pair(chips - 1, state)

    stats[t, 0:1] = row_max
    stats[t, 1:2] = row_sum
    stats[t, 2:3] = matched

    def st_copy(i):
        return remote(stats.at[t], stats.at[t], st_send.at[i], st_recv.at[t], (me, peer(i)))

    def st_from(i):
        slot = stats.at[peer(i)]
        return remote(slot, slot, st_send.at[i], st_recv.at[peer(i)], (me, peer(i)))

    for i in range(1, groups):
        st_copy(i).start()
    for i in range(1, groups):
        st_from(i).wait_recv()
    best = stats[0, 0:1]
    for s in range(1, groups):
        best = jnp.maximum(best, stats[s, 0:1])
    total = jnp.zeros_like(best)
    matched = jnp.zeros_like(best)
    for s in range(groups):
        total = total + stats[s, 1:2] * jnp.exp(stats[s, 0:1] - best)
        matched = matched + stats[s, 2:3]
    log_total = best + jnp.log(total)
    loss_ref[...] = log_total - matched

    def weigh(index, carried):
        weights[index] = jnp.exp(scores[index] - log_total).astype(jnp.bfloat16)
        return carried

    def target(i):
        return lax.rem(chip + 2 * chips - 1 - i, chips) * 2

    def key_part(index):
        return jnp.dot(weights[index], qhat[...], preferred_element_type=jnp.float32)

    def sb_copy(i):
        return remote(sib_out.at[i], sib_in.at[i], sb_send.at[i], sb_recv.at[i], (sibling, t))

    def rg_copy(i, h):
        span = pl.ds(h * half, half)
        return remote(
            sib_in.at[i, span], ring_in.at[i, span], rg_send.at[i, h], rg_recv.at[i, h], (right, t)
        )

    def hand_over(i, carried):
        sib_out[i] = key_part(target(i) + other).astype(jnp.bfloat16)
        sb_copy(i).start()
        return carried

    def ring_first():
        value = key_part(target(0) + core)
        sb_copy(0).wait_recv()
        for h in range(HALVES):
            span = slice(h * half, (h + 1) * half)
            sib_in[0, span] = (value[span] + sib_in[0, span].astype(jnp.float32)).astype(jnp.bfloat16)
            rg_copy(0, h).start()

    def ring_next(i, carried):
        value = key_part(target(i) + core)
        sb_copy(i).wait_recv()
        for h in range(HALVES):
            span = slice(h * half, (h + 1) * half)
            both = value[span] + sib_in[i, span].astype(jnp.float32)
            rg_copy(i - 1, h).wait_recv()
            sib_in[i, span] = (both + ring_in[i - 1, span].astype(jnp.float32)).astype(jnp.bfloat16)
            rg_copy(i, h).start()
        return carried

    def weigh_pair(i, carried):
        weigh(target(i) + other, 0)
        hand_over(i, 0)
        return weigh(target(i) + core, carried)

    weigh_pair(0, 0)
    ring_first()
    lax.fori_loop(1, chips - 1, weigh_pair, 0)
    weigh(sibling, 0)
    hand_over(chips - 1, 0)
    weights[me] = (jnp.exp(scores[me] - log_total) - positive_mask()).astype(jnp.bfloat16)

    def query_part(p):
        span = pl.ds(pl.multiple_of(p * part, part), part)
        chosen = weights[:, :, span].reshape(2 * chips * part, part)
        keys = kall[...].reshape(2 * chips * part, groups * feats)
        return lax.dot_general(
            chosen, keys, (((0,), (0,)), ((), ())), preferred_element_type=jnp.float32
        )

    def gq_copy(i):
        return remote(gq_out.at[i - 1], gq_in.at[i - 1], gq_send.at[i - 1], gq_recv.at[i - 1], (me, peer(i)))

    def query_send(i, carried):
        gq_out[i - 1] = query_part(peer(i)).astype(jnp.bfloat16)
        gq_copy(i).start()
        return carried

    query_send(1, 0)
    lax.fori_loop(1, min(2, chips - 1), ring_next, 0)
    lax.fori_loop(2, groups, query_send, 0)
    gq_ref[...] = query_part(t)
    lax.fori_loop(2, chips - 1, ring_next, 0)

    def unnormalized(grad, unit, inverse):
        grad = grad * SCALE
        return (grad - unit * jnp.sum(unit * grad, axis=1, keepdims=True)) * inverse

    value = gq_ref[...]
    for i in range(1, groups):
        gq_copy(i).wait_recv()
        value = value + gq_in[i - 1].astype(jnp.float32)
    own_rows = pl.ds(pl.multiple_of(t * part, part), part)
    blocks = [qraw[s, own_rows].astype(jnp.float32) for s in range(groups)]
    inverse = inverse_magnitude(blocks)
    gq_ref[...] = unnormalized(value, jnp.concatenate(blocks, axis=1) * inverse, inverse)

    value = key_part(me)
    sb_copy(chips - 1).wait_recv()
    value = value + sib_in[chips - 1].astype(jnp.float32)
    for h in range(HALVES):
        rg_copy(chips - 2, h).wait_recv()
    value = value + ring_in[chips - 2].astype(jnp.float32)
    blocks = [kraw[s].astype(jnp.float32) for s in range(groups)]
    inverse = inverse_magnitude(blocks)
    gk_ref[...] = unnormalized(value, jnp.concatenate(blocks, axis=1) * inverse, inverse)

    for i in range(1, groups):
        kx_copy(i).wait_send()
        qx_copy(i).wait_send()
        st_copy(i).wait_send()
        gq_copy(i).wait_send()
    for s in range(chips):
        sb_copy(s).wait_send()
        for h in range(HALVES):
            fwd_copy(s, h).wait_send()
            if s < chips - 1:
                ring_copy(s, h).wait_send()
                rg_copy(s, h).wait_send()


PIECES = 4


def deliver(loss_in, gq_in, gk_in, loss_out, gq_out, gk_out, sems, loss_sem):
    part = gq_out.shape[0]
    start = pl.multiple_of(lax.axis_index("tensor") * part, part)
    copies = [pltpu.make_async_copy(loss_in.at[:, pl.ds(start, part)], loss_out, loss_sem)]
    for a, (src, dst) in enumerate(((gq_in, gq_out), (gk_in, gk_out))):
        for p in range(PIECES):
            span = pl.ds(p * (part // PIECES), part // PIECES)
            copies.append(pltpu.make_async_copy(src.at[span], dst.at[span], sems.at[a, p]))
    for copy in copies:
        copy.start()
    for copy in copies:
        copy.wait()


def body(queries, keys, projection, positives):
    dp, groups = lax.axis_size("dp"), lax.axis_size("tensor")
    chips = dp // 2
    rows = queries.shape[0]
    part = rows // groups
    feats = projection.shape[1]
    width = feats * groups
    embed = queries.shape[1]
    slots = min(STAGE_BYTES // (rows * DEPTH * 2), embed // DEPTH)
    bf16, f32 = jnp.bfloat16, jnp.float32
    vmem, dma = pltpu.VMEM, pltpu.SemaphoreType.DMA
    spec = pl.BlockSpec(memory_space=pltpu.VMEM)
    loss, grad_q, grad_k = pl.pallas_call(
        functools.partial(kernel, chips, groups),
        out_shape=(
            jax.ShapeDtypeStruct((1, rows), f32),
            jax.ShapeDtypeStruct((part, width), f32),
            jax.ShapeDtypeStruct((part, width), f32),
        ),
        in_specs=[pl.BlockSpec(memory_space=pl.ANY)] * 3 + [spec],
        out_specs=(spec,) * 3,
        scratch_shapes=[
            vmem((slots, rows, DEPTH), bf16),
            vmem((embed, feats), bf16),
            vmem((rows, feats), bf16),
            vmem((groups, part, feats), bf16),
            vmem((dp, part, width), bf16),
            vmem((groups, rows, feats), bf16),
            vmem((rows, width), bf16),
            vmem((dp, part, rows), f32),
            vmem((dp, part, rows), bf16),
            vmem((groups, 8, rows), f32),
            vmem((chips, part, width), bf16),
            vmem((chips, part, width), bf16),
            vmem((chips - 1, part, width), bf16),
            vmem((groups - 1, part, width), bf16),
            vmem((groups - 1, part, width), bf16),
            dma((slots,)), dma((embed // DEPTH,)),
            dma((groups,)), dma((groups,)), dma((groups,)), dma((groups,)),
            dma((chips, HALVES)), dma((chips, HALVES)), dma((dp, HALVES)),
            dma((groups,)), dma((groups,)),
            dma((chips,)), dma((chips,)),
            dma((chips, HALVES)), dma((chips, HALVES)),
            dma((groups,)), dma((groups,)),
        ],
        compiler_params=pltpu.CompilerParams(
            collective_id=0, has_side_effects=True, vmem_limit_bytes=62 * 1024 * 1024
        ),
        cost_estimate=pl.CostEstimate(
            flops=8 * rows * dp * part * width + 4 * rows * embed * feats,
            bytes_accessed=(4 * rows + 2 * feats) * embed + 8 * part * width,
            transcendentals=2 * rows * dp * part,
        ),
    )(queries, keys, projection, positives)
    whole = pl.BlockSpec(memory_space=pl.ANY)
    pair_loss, grad_q, grad_k = pl.pallas_call(
        deliver,
        out_shape=(
            jax.ShapeDtypeStruct((1, part), f32),
            jax.ShapeDtypeStruct((part, width), f32),
            jax.ShapeDtypeStruct((part, width), f32),
        ),
        in_specs=[whole] * 3,
        out_specs=(whole,) * 3,
        scratch_shapes=[dma((2, PIECES)), dma],
        compiler_params=pltpu.CompilerParams(vmem_limit_bytes=62 * 1024 * 1024),
        cost_estimate=pl.CostEstimate(
            flops=0, bytes_accessed=16 * part * width, transcendentals=0
        ),
    )(loss, grad_q, grad_k)
    return (pair_loss.reshape(part), grad_q, grad_k)


def solution(mesh):
    in_specs = (P("dp", None), P("dp", None), P(None, "tensor"), P("dp", None))
    out_specs = (P(("dp", "tensor")), P(("dp", "tensor"), None), P(("dp", "tensor"), None))
    return jax.shard_map(body, mesh=mesh, in_specs=in_specs, out_specs=out_specs, check_vma=False)
```

```python
import functools

import jax
import jax.numpy as jnp
from jax import lax
from jax.experimental import pallas as pl
from jax.experimental.pallas import tpu as pltpu
from jax.sharding import PartitionSpec as P

SCALE = 100.0
EPSILON = 1e-06
MESH = pl.DeviceIdType.MESH
HALVES = 2
DEPTH = 512
STAGE_BYTES = 4 * 1024 * 1024


def kernel(
    chips, groups, q_hbm, k_hbm, w_hbm, pos_ref, loss_ref, gq_ref, gk_ref,
    stage, w_in, kfeat, kraw, kall, qraw, qhat, scores, weights, stats,
    sib_out, sib_in, ring_in, gq_out, gq_in, stage_sem, w_sem,
    kx_send, kx_recv, qx_send, qx_recv, ring_send, fwd_send, k_recv,
    st_send, st_recv, sb_send, sb_recv, rg_send, rg_recv, gq_send, gq_recv,
):
    rows, feats = kfeat.shape
    slots, steps = stage.shape[0], w_in.shape[0] // DEPTH
    part = rows // groups
    half = part // HALVES
    me = lax.axis_index("dp")
    t = lax.axis_index("tensor")
    chip, core = me // 2, me % 2
    other = 1 - core
    sibling = chip * 2 + other
    right = lax.rem(chip + 1, chips) * 2 + core
    left = lax.rem(chip + chips - 1, chips) * 2 + core

    def peer(i):
        return lax.rem(t + i, groups)

    def remote(src, dst, send, recv, device):
        return pltpu.make_async_remote_copy(
            src_ref=src, dst_ref=dst, send_sem=send, recv_sem=recv,
            device_id=device, device_id_type=MESH,
        )

    barrier = pltpu.get_barrier_semaphore()
    for i in range(1, groups):
        pl.semaphore_signal(barrier, inc=1, device_id=(me, peer(i)), device_id_type=MESH)
    for device in (sibling, right, left):
        pl.semaphore_signal(barrier, inc=1, device_id=(device, t), device_id_type=MESH)

    def w_copy(c):
        span = pl.ds(c * DEPTH, DEPTH)
        return pltpu.make_async_copy(w_hbm.at[span], w_in.at[span], w_sem.at[c])

    def stage_copy(c):
        source_ref = k_hbm if c < steps else q_hbm
        span = pl.ds((c % steps) * DEPTH, DEPTH)
        return pltpu.make_async_copy(
            source_ref.at[:, span], stage.at[c % slots], stage_sem.at[c % slots]
        )

    for c in range(max(steps, slots)):
        if c < steps:
            w_copy(c).start()
        if c < slots:
            stage_copy(c).start()

    def project(first):
        total = None
        for c in range(steps):
            if first == 0:
                w_copy(c).wait()
            stage_copy(first + c).wait()
            term = jnp.dot(
                stage[(first + c) % slots], w_in[c * DEPTH : (c + 1) * DEPTH],
                preferred_element_type=jnp.float32,
            )
            total = term if total is None else total + term
            if first + c + slots < 2 * steps:
                stage_copy(first + c + slots).start()
        return total.astype(jnp.bfloat16)

    kfeat[...] = project(0)
    pl.semaphore_wait(barrier, groups + 2)

    def kx_copy(i):
        rows_of = pl.ds(pl.multiple_of(peer(i) * part, part), part)
        return remote(kfeat.at[rows_of], kraw.at[t], kx_send.at[i], kx_recv.at[t], (me, peer(i)))

    def kx_from(i):
        slot = kraw.at[peer(i)]
        return remote(slot, slot, kx_send.at[i], kx_recv.at[peer(i)], (me, peer(i)))

    def qx_copy(i):
        return remote(qraw.at[t], qraw.at[t], qx_send.at[i], qx_recv.at[t], (me, peer(i)))

    def qx_from(i):
        slot = qraw.at[peer(i)]
        return remote(slot, slot, qx_send.at[i], qx_recv.at[peer(i)], (me, peer(i)))

    for i in range(1, groups):
        kx_copy(i).start()
    kraw[t] = kfeat[pl.ds(pl.multiple_of(t * part, part), part)]
    qraw[t] = project(steps)
    for i in range(1, groups):
        kx_from(i).wait_recv()

    def inverse_magnitude(blocks):
        total = blocks[0] * blocks[0]
        for block in blocks[1:]:
            total = total + block * block
        return lax.rsqrt(jnp.sum(total, axis=1, keepdims=True) + EPSILON)

    entries = [kraw[s].astype(jnp.float32) for s in range(groups)]
    k_inverse = inverse_magnitude(entries)
    for s in range(groups):
        kall[me, :, s * feats : (s + 1) * feats] = (entries[s] * k_inverse).astype(
            jnp.bfloat16
        )

    def source(s):
        return lax.rem(chip + chips - s, chips) * 2

    def ring_copy(s, h):
        slot = kall.at[source(s) + core, pl.ds(h * half, half)]
        return remote(slot, slot, ring_send.at[s, h], k_recv.at[source(s) + core, h], (right, t))

    def fwd_copy(s, h):
        slot = kall.at[source(s) + core, pl.ds(h * half, half)]
        return remote(slot, slot, fwd_send.at[s, h], k_recv.at[source(s) + core, h], (sibling, t))

    def k_from(index, h):
        slot = kall.at[index, pl.ds(h * half, half)]
        return remote(slot, slot, ring_send.at[0, h], k_recv.at[index, h], (right, t))

    def forward(s):
        for h in range(HALVES):
            if s > 0:
                k_from(source(s) + core, h).wait_recv()
            if s < chips - 1:
                ring_copy(s, h).start()
            fwd_copy(s, h).start()

    forward(0)
    for i in range(1, groups):
        qx_copy(i).start()
    for s in range(1, chips - 1):
        forward(s)

    for i in range(1, groups):
        qx_from(i).wait_recv()

    def normalize_rows(p, carried):
        span = pl.ds(pl.multiple_of(p * part, part), part)
        blocks = [qraw[s, span].astype(jnp.float32) for s in range(groups)]
        inverse = inverse_magnitude(blocks)
        for s in range(groups):
            qhat[span, s * feats : (s + 1) * feats] = (blocks[s] * inverse).astype(jnp.bfloat16)
        return carried

    lax.fori_loop(0, groups, normalize_rows, 0)

    def score(index):
        block = SCALE * lax.dot_general(
            kall[index], qhat[...], (((1,), (1,)), ((), ())), preferred_element_type=jnp.float32
        )
        scores[index] = block
        return block

    def fold(index, state):
        row_max, row_sum = state
        block = score(index)
        new_max = jnp.maximum(row_max, jnp.max(block, axis=0, keepdims=True))
        row_sum = row_sum * jnp.exp(row_max - new_max) + jnp.sum(
            jnp.exp(block - new_max), axis=0, keepdims=True
        )
        return (new_max, row_sum)

    def positive_mask():
        key_index = lax.broadcasted_iota(jnp.int32, (part, rows), 0)
        return (key_index == pos_ref[...] - t * part).astype(jnp.float32)

    own = score(me)
    row_max = jnp.max(own, axis=0, keepdims=True)
    row_sum = jnp.sum(jnp.exp(own - row_max), axis=0, keepdims=True)
    matched = jnp.sum(own * positive_mask(), axis=0, keepdims=True)

    def from_sibling(s):
        for h in range(HALVES):
            k_from(source(s) + other, h).wait_recv()

    def fold_pair(s, state):
        state = fold(source(s) + core, state)
        from_sibling(s)
        return fold(source(s) + other, state)

    from_sibling(0)
    state = fold(source(0) + other, (row_max, row_sum))
    state = lax.fori_loop(1, chips - 1, fold_pair, state)
    forward(chips - 1)
    row_max, row_sum = fold_pair(chips - 1, state)

    stats[t, 0:1] = row_max
    stats[t, 1:2] = row_sum
    stats[t, 2:3] = matched

    def st_copy(i):
        return remote(stats.at[t], stats.at[t], st_send.at[i], st_recv.at[t], (me, peer(i)))

    def st_from(i):
        slot = stats.at[peer(i)]
        return remote(slot, slot, st_send.at[i], st_recv.at[peer(i)], (me, peer(i)))

    for i in range(1, groups):
        st_copy(i).start()
    for i in range(1, groups):
        st_from(i).wait_recv()
    best = stats[0, 0:1]
    for s in range(1, groups):
        best = jnp.maximum(best, stats[s, 0:1])
    total = jnp.zeros_like(best)
    matched = jnp.zeros_like(best)
    for s in range(groups):
        total = total + stats[s, 1:2] * jnp.exp(stats[s, 0:1] - best)
        matched = matched + stats[s, 2:3]
    log_total = best + jnp.log(total)
    loss_ref[...] = log_total - matched

    def weigh(index, carried):
        weights[index] = jnp.exp(scores[index] - log_total).astype(jnp.bfloat16)
        return carried

    def target(i):
        return lax.rem(chip + 2 * chips - 1 - i, chips) * 2

    def key_part(index):
        return jnp.dot(weights[index], qhat[...], preferred_element_type=jnp.float32)

    def sb_copy(i):
        return remote(sib_out.at[i], sib_in.at[i], sb_send.at[i], sb_recv.at[i], (sibling, t))

    def rg_copy(i, h):
        span = pl.ds(h * half, half)
        return remote(
            sib_in.at[i, span], ring_in.at[i, span], rg_send.at[i, h], rg_recv.at[i, h], (right, t)
        )

    def hand_over(i, carried):
        sib_out[i] = key_part(target(i) + other).astype(jnp.bfloat16)
        sb_copy(i).start()
        return carried

    def ring_first():
        value = key_part(target(0) + core)
        sb_copy(0).wait_recv()
        for h in range(HALVES):
            span = slice(h * half, (h + 1) * half)
            sib_in[0, span] = (value[span] + sib_in[0, span].astype(jnp.float32)).astype(jnp.bfloat16)
            rg_copy(0, h).start()

    def ring_next(i, carried):
        value = key_part(target(i) + core)
        sb_copy(i).wait_recv()
        for h in range(HALVES):
            span = slice(h * half, (h + 1) * half)
            both = value[span] + sib_in[i, span].astype(jnp.float32)
            rg_copy(i - 1, h).wait_recv()
            sib_in[i, span] = (both + ring_in[i - 1, span].astype(jnp.float32)).astype(jnp.bfloat16)
            rg_copy(i, h).start()
        return carried

    def weigh_pair(i, carried):
        weigh(target(i) + other, 0)
        hand_over(i, 0)
        return weigh(target(i) + core, carried)

    weigh_pair(0, 0)
    ring_first()
    lax.fori_loop(1, chips - 1, weigh_pair, 0)
    weigh(sibling, 0)
    hand_over(chips - 1, 0)
    weights[me] = (jnp.exp(scores[me] - log_total) - positive_mask()).astype(jnp.bfloat16)

    def query_part(p):
        span = pl.ds(pl.multiple_of(p * part, part), part)
        chosen = weights[:, :, span].reshape(2 * chips * part, part)
        keys = kall[...].reshape(2 * chips * part, groups * feats)
        return lax.dot_general(
            chosen, keys, (((0,), (0,)), ((), ())), preferred_element_type=jnp.float32
        )

    def gq_copy(i):
        return remote(gq_out.at[i - 1], gq_in.at[i - 1], gq_send.at[i - 1], gq_recv.at[i - 1], (me, peer(i)))

    def query_send(i, carried):
        gq_out[i - 1] = query_part(peer(i)).astype(jnp.bfloat16)
        gq_copy(i).start()
        return carried

    query_send(1, 0)
    lax.fori_loop(1, min(2, chips - 1), ring_next, 0)
    lax.fori_loop(2, groups, query_send, 0)
    lax.fori_loop(2, chips - 1, ring_next, 0)
    gq_ref[...] = query_part(t)

    def unnormalized(grad, unit, inverse):
        grad = grad * SCALE
        return (grad - unit * jnp.sum(unit * grad, axis=1, keepdims=True)) * inverse

    value = gq_ref[...]
    for i in range(1, groups):
        gq_copy(i).wait_recv()
        value = value + gq_in[i - 1].astype(jnp.float32)
    own_rows = pl.ds(pl.multiple_of(t * part, part), part)
    blocks = [qraw[s, own_rows].astype(jnp.float32) for s in range(groups)]
    inverse = inverse_magnitude(blocks)
    gq_ref[...] = unnormalized(value, jnp.concatenate(blocks, axis=1) * inverse, inverse)

    value = key_part(me)
    sb_copy(chips - 1).wait_recv()
    value = value + sib_in[chips - 1].astype(jnp.float32)
    for h in range(HALVES):
        rg_copy(chips - 2, h).wait_recv()
    value = value + ring_in[chips - 2].astype(jnp.float32)
    blocks = [kraw[s].astype(jnp.float32) for s in range(groups)]
    inverse = inverse_magnitude(blocks)
    gk_ref[...] = unnormalized(value, jnp.concatenate(blocks, axis=1) * inverse, inverse)

    for i in range(1, groups):
        kx_copy(i).wait_send()
        qx_copy(i).wait_send()
        st_copy(i).wait_send()
        gq_copy(i).wait_send()
    for s in range(chips):
        sb_copy(s).wait_send()
        for h in range(HALVES):
            fwd_copy(s, h).wait_send()
            if s < chips - 1:
                ring_copy(s, h).wait_send()
                rg_copy(s, h).wait_send()


PIECES = 4


def deliver(
    loss_in, gq_in, gk_in, loss_out, gq_out, gk_out, loss_held, held, in_sems, out_sems, loss_sems
):
    part = gq_out.shape[0]
    start = pl.multiple_of(lax.axis_index("tensor") * part, part)
    copies = []
    for a, (src, dst) in enumerate(((gq_in, gq_out), (gk_in, gk_out))):
        for p in range(PIECES):
            span = pl.ds(p * (part // PIECES), part // PIECES)
            slot = held.at[a, span]
            copies.append((
                pltpu.make_async_copy(src.at[span], slot, in_sems.at[a, p]),
                pltpu.make_async_copy(slot, dst.at[span], out_sems.at[a, p]),
            ))
    copies.append((
        pltpu.make_async_copy(loss_in.at[:, pl.ds(start, part)], loss_held, loss_sems.at[0]),
        pltpu.make_async_copy(loss_held, loss_out, loss_sems.at[1]),
    ))
    for arrive, _ in copies:
        arrive.start()
    for arrive, leave in copies:
        arrive.wait()
        leave.start()
    for _, leave in copies:
        leave.wait()


def body(queries, keys, projection, positives):
    dp, groups = lax.axis_size("dp"), lax.axis_size("tensor")
    chips = dp // 2
    rows = queries.shape[0]
    part = rows // groups
    feats = projection.shape[1]
    width = feats * groups
    embed = queries.shape[1]
    slots = min(STAGE_BYTES // (rows * DEPTH * 2), embed // DEPTH)
    bf16, f32 = jnp.bfloat16, jnp.float32
    vmem, dma = pltpu.VMEM, pltpu.SemaphoreType.DMA
    spec = pl.BlockSpec(memory_space=pltpu.VMEM)
    loss, grad_q, grad_k = pl.pallas_call(
        functools.partial(kernel, chips, groups),
        out_shape=(
            jax.ShapeDtypeStruct((1, rows), f32),
            jax.ShapeDtypeStruct((part, width), f32),
            jax.ShapeDtypeStruct((part, width), f32),
        ),
        in_specs=[pl.BlockSpec(memory_space=pl.ANY)] * 3 + [spec],
        out_specs=(spec,) * 3,
        scratch_shapes=[
            vmem((slots, rows, DEPTH), bf16),
            vmem((embed, feats), bf16),
            vmem((rows, feats), bf16),
            vmem((groups, part, feats), bf16),
            vmem((dp, part, width), bf16),
            vmem((groups, rows, feats), bf16),
            vmem((rows, width), bf16),
            vmem((dp, part, rows), f32),
            vmem((dp, part, rows), bf16),
            vmem((groups, 8, rows), f32),
            vmem((chips, part, width), bf16),
            vmem((chips, part, width), bf16),
            vmem((chips - 1, part, width), bf16),
            vmem((groups - 1, part, width), bf16),
            vmem((groups - 1, part, width), bf16),
            dma((slots,)), dma((embed // DEPTH,)),
            dma((groups,)), dma((groups,)), dma((groups,)), dma((groups,)),
            dma((chips, HALVES)), dma((chips, HALVES)), dma((dp, HALVES)),
            dma((groups,)), dma((groups,)),
            dma((chips,)), dma((chips,)),
            dma((chips, HALVES)), dma((chips, HALVES)),
            dma((groups,)), dma((groups,)),
        ],
        compiler_params=pltpu.CompilerParams(
            collective_id=0, has_side_effects=True, vmem_limit_bytes=62 * 1024 * 1024
        ),
        cost_estimate=pl.CostEstimate(
            flops=8 * rows * dp * part * width + 4 * rows * embed * feats,
            bytes_accessed=(4 * rows + 2 * feats) * embed + 8 * part * width,
            transcendentals=2 * rows * dp * part,
        ),
    )(queries, keys, projection, positives)
    whole = pl.BlockSpec(memory_space=pl.ANY)
    pair_loss, grad_q, grad_k = pl.pallas_call(
        deliver,
        out_shape=(
            jax.ShapeDtypeStruct((1, part), f32),
            jax.ShapeDtypeStruct((part, width), f32),
            jax.ShapeDtypeStruct((part, width), f32),
        ),
        in_specs=[whole] * 3,
        out_specs=(whole,) * 3,
        scratch_shapes=[
            vmem((1, part), f32), vmem((2, part, width), f32),
            dma((2, PIECES)), dma((2, PIECES)), dma((2,)),
        ],
        compiler_params=pltpu.CompilerParams(vmem_limit_bytes=62 * 1024 * 1024),
        cost_estimate=pl.CostEstimate(
            flops=0, bytes_accessed=16 * part * width, transcendentals=0
        ),
    )(loss, grad_q, grad_k)
    return (pair_loss.reshape(part), grad_q, grad_k)


def solution(mesh):
    in_specs = (P("dp", None), P("dp", None), P(None, "tensor"), P("dp", None))
    out_specs = (P(("dp", "tensor")), P(("dp", "tensor"), None), P(("dp", "tensor"), None))
    return jax.shard_map(body, mesh=mesh, in_specs=in_specs, out_specs=out_specs, check_vma=False)
```

```python
import functools

import jax
import jax.numpy as jnp
from jax import lax
from jax.experimental import pallas as pl
from jax.experimental.pallas import tpu as pltpu
from jax.sharding import PartitionSpec as P

SCALE = 100.0
EPSILON = 1e-06
MESH = pl.DeviceIdType.MESH
HALVES = 2
DEPTH = 512
STAGE_BYTES = 4 * 1024 * 1024


def kernel(
    chips, groups, q_hbm, k_hbm, w_hbm, pos_ref, loss_ref, gq_ref, gk_ref,
    stage, w_in, kfeat, kraw, kall, qraw, qhat, scores, weights, stats,
    sib_out, sib_in, ring_in, gq_out, gq_in, stage_sem, w_sem,
    kx_send, kx_recv, qx_send, qx_recv, ring_send, fwd_send, k_recv,
    st_send, st_recv, sb_send, sb_recv, rg_send, rg_recv, gq_send, gq_recv,
):
    rows, feats = kfeat.shape
    slots, steps = stage.shape[0], w_in.shape[0] // DEPTH
    part = rows // groups
    half = part // HALVES
    me = lax.axis_index("dp")
    t = lax.axis_index("tensor")
    chip, core = me // 2, me % 2
    other = 1 - core
    sibling = chip * 2 + other
    right = lax.rem(chip + chips + 1 - 2 * core, chips) * 2 + core
    left = lax.rem(chip + chips - 1 + 2 * core, chips) * 2 + core

    def peer(i):
        return lax.rem(t + i, groups)

    def remote(src, dst, send, recv, device):
        return pltpu.make_async_remote_copy(
            src_ref=src, dst_ref=dst, send_sem=send, recv_sem=recv,
            device_id=device, device_id_type=MESH,
        )

    barrier = pltpu.get_barrier_semaphore()
    for i in range(1, groups):
        pl.semaphore_signal(barrier, inc=1, device_id=(me, peer(i)), device_id_type=MESH)
    for device in (sibling, right, left):
        pl.semaphore_signal(barrier, inc=1, device_id=(device, t), device_id_type=MESH)

    def w_copy(c):
        span = pl.ds(c * DEPTH, DEPTH)
        return pltpu.make_async_copy(w_hbm.at[span], w_in.at[span], w_sem.at[c])

    def stage_copy(c):
        source_ref = k_hbm if c < steps else q_hbm
        span = pl.ds((c % steps) * DEPTH, DEPTH)
        return pltpu.make_async_copy(
            source_ref.at[:, span], stage.at[c % slots], stage_sem.at[c % slots]
        )

    for c in range(max(steps, slots)):
        if c < steps:
            w_copy(c).start()
        if c < slots:
            stage_copy(c).start()

    def project(first):
        total = None
        for c in range(steps):
            if first == 0:
                w_copy(c).wait()
            stage_copy(first + c).wait()
            term = jnp.dot(
                stage[(first + c) % slots], w_in[c * DEPTH : (c + 1) * DEPTH],
                preferred_element_type=jnp.float32,
            )
            total = term if total is None else total + term
            if first + c + slots < 2 * steps:
                stage_copy(first + c + slots).start()
        return total.astype(jnp.bfloat16)

    kfeat[...] = project(0)
    pl.semaphore_wait(barrier, groups + 2)

    def kx_copy(i):
        rows_of = pl.ds(pl.multiple_of(peer(i) * part, part), part)
        return remote(kfeat.at[rows_of], kraw.at[t], kx_send.at[i], kx_recv.at[t], (me, peer(i)))

    def kx_from(i):
        slot = kraw.at[peer(i)]
        return remote(slot, slot, kx_send.at[i], kx_recv.at[peer(i)], (me, peer(i)))

    def qx_copy(i):
        return remote(qraw.at[t], qraw.at[t], qx_send.at[i], qx_recv.at[t], (me, peer(i)))

    def qx_from(i):
        slot = qraw.at[peer(i)]
        return remote(slot, slot, qx_send.at[i], qx_recv.at[peer(i)], (me, peer(i)))

    for i in range(1, groups):
        kx_copy(i).start()
    kraw[t] = kfeat[pl.ds(pl.multiple_of(t * part, part), part)]
    qraw[t] = project(steps)
    for i in range(1, groups):
        kx_from(i).wait_recv()

    def inverse_magnitude(blocks):
        total = blocks[0] * blocks[0]
        for block in blocks[1:]:
            total = total + block * block
        return lax.rsqrt(jnp.sum(total, axis=1, keepdims=True) + EPSILON)

    entries = [kraw[s].astype(jnp.float32) for s in range(groups)]
    k_inverse = inverse_magnitude(entries)
    for s in range(groups):
        kall[me, :, s * feats : (s + 1) * feats] = (entries[s] * k_inverse).astype(
            jnp.bfloat16
        )

    def source(s, c):
        return lax.rem(chip + chips - s + 2 * s * c, chips) * 2 + c

    def ring_copy(s, h):
        slot = kall.at[source(s, core), pl.ds(h * half, half)]
        return remote(slot, slot, ring_send.at[s, h], k_recv.at[source(s, core), h], (right, t))

    def fwd_copy(s, h):
        slot = kall.at[source(s, core), pl.ds(h * half, half)]
        return remote(slot, slot, fwd_send.at[s, h], k_recv.at[source(s, core), h], (sibling, t))

    def k_from(index, h):
        slot = kall.at[index, pl.ds(h * half, half)]
        return remote(slot, slot, ring_send.at[0, h], k_recv.at[index, h], (right, t))

    def forward(s):
        for h in range(HALVES):
            if s > 0:
                k_from(source(s, core), h).wait_recv()
            if s < chips - 1:
                ring_copy(s, h).start()
            fwd_copy(s, h).start()

    forward(0)
    for i in range(1, groups):
        qx_copy(i).start()
    for s in range(1, chips - 1):
        forward(s)

    for i in range(1, groups):
        qx_from(i).wait_recv()

    def normalize_rows(p, carried):
        span = pl.ds(pl.multiple_of(p * part, part), part)
        blocks = [qraw[s, span].astype(jnp.float32) for s in range(groups)]
        inverse = inverse_magnitude(blocks)
        for s in range(groups):
            qhat[span, s * feats : (s + 1) * feats] = (blocks[s] * inverse).astype(jnp.bfloat16)
        return carried

    lax.fori_loop(0, groups, normalize_rows, 0)

    def score(index):
        block = SCALE * lax.dot_general(
            kall[index], qhat[...], (((1,), (1,)), ((), ())), preferred_element_type=jnp.float32
        )
        scores[index] = block
        return block

    def fold(index, state):
        row_max, row_sum = state
        block = score(index)
        new_max = jnp.maximum(row_max, jnp.max(block, axis=0, keepdims=True))
        row_sum = row_sum * jnp.exp(row_max - new_max) + jnp.sum(
            jnp.exp(block - new_max), axis=0, keepdims=True
        )
        return (new_max, row_sum)

    def positive_mask():
        key_index = lax.broadcasted_iota(jnp.int32, (part, rows), 0)
        return (key_index == pos_ref[...] - t * part).astype(jnp.float32)

    own = score(me)
    row_max = jnp.max(own, axis=0, keepdims=True)
    row_sum = jnp.sum(jnp.exp(own - row_max), axis=0, keepdims=True)
    matched = jnp.sum(own * positive_mask(), axis=0, keepdims=True)

    def from_sibling(s):
        for h in range(HALVES):
            k_from(source(s, other), h).wait_recv()

    def fold_pair(s, state):
        state = fold(source(s, core), state)
        from_sibling(s)
        return fold(source(s, other), state)

    from_sibling(0)
    state = fold(source(0, other), (row_max, row_sum))
    state = lax.fori_loop(1, chips - 1, fold_pair, state)
    forward(chips - 1)
    row_max, row_sum = fold_pair(chips - 1, state)

    stats[t, 0:1] = row_max
    stats[t, 1:2] = row_sum
    stats[t, 2:3] = matched

    def st_copy(i):
        return remote(stats.at[t], stats.at[t], st_send.at[i], st_recv.at[t], (me, peer(i)))

    def st_from(i):
        slot = stats.at[peer(i)]
        return remote(slot, slot, st_send.at[i], st_recv.at[peer(i)], (me, peer(i)))

    for i in range(1, groups):
        st_copy(i).start()
    for i in range(1, groups):
        st_from(i).wait_recv()
    best = stats[0, 0:1]
    for s in range(1, groups):
        best = jnp.maximum(best, stats[s, 0:1])
    total = jnp.zeros_like(best)
    matched = jnp.zeros_like(best)
    for s in range(groups):
        total = total + stats[s, 1:2] * jnp.exp(stats[s, 0:1] - best)
        matched = matched + stats[s, 2:3]
    log_total = best + jnp.log(total)
    loss_ref[...] = log_total - matched

    def weigh(index, carried):
        weights[index] = jnp.exp(scores[index] - log_total).astype(jnp.bfloat16)
        return carried

    def target(i, c):
        return lax.rem(chip + 2 * chips - (1 + i) * (1 - 2 * c), chips) * 2 + c

    def key_part(index):
        return jnp.dot(weights[index], qhat[...], preferred_element_type=jnp.float32)

    def sb_copy(i):
        return remote(sib_out.at[i], sib_in.at[i], sb_send.at[i], sb_recv.at[i], (sibling, t))

    def rg_copy(i, h):
        span = pl.ds(h * half, half)
        return remote(
            sib_in.at[i, span], ring_in.at[i, span], rg_send.at[i, h], rg_recv.at[i, h], (right, t)
        )

    def hand_over(i, carried):
        sib_out[i] = key_part(target(i, other)).astype(jnp.bfloat16)
        sb_copy(i).start()
        return carried

    def ring_first():
        value = key_part(target(0, core))
        sb_copy(0).wait_recv()
        for h in range(HALVES):
            span = slice(h * half, (h + 1) * half)
            sib_in[0, span] = (value[span] + sib_in[0, span].astype(jnp.float32)).astype(jnp.bfloat16)
            rg_copy(0, h).start()

    def ring_next(i, carried):
        value = key_part(target(i, core))
        sb_copy(i).wait_recv()
        for h in range(HALVES):
            span = slice(h * half, (h + 1) * half)
            both = value[span] + sib_in[i, span].astype(jnp.float32)
            rg_copy(i - 1, h).wait_recv()
            sib_in[i, span] = (both + ring_in[i - 1, span].astype(jnp.float32)).astype(jnp.bfloat16)
            rg_copy(i, h).start()
        return carried

    def weigh_pair(i, carried):
        weigh(target(i, other), 0)
        hand_over(i, 0)
        return weigh(target(i, core), carried)

    weigh_pair(0, 0)
    ring_first()
    lax.fori_loop(1, chips - 1, weigh_pair, 0)
    weigh(sibling, 0)
    hand_over(chips - 1, 0)
    weights[me] = (jnp.exp(scores[me] - log_total) - positive_mask()).astype(jnp.bfloat16)

    def query_part(p):
        span = pl.ds(pl.multiple_of(p * part, part), part)
        chosen = weights[:, :, span].reshape(2 * chips * part, part)
        keys = kall[...].reshape(2 * chips * part, groups * feats)
        return lax.dot_general(
            chosen, keys, (((0,), (0,)), ((), ())), preferred_element_type=jnp.float32
        )

    def gq_copy(i):
        return remote(gq_out.at[i - 1], gq_in.at[i - 1], gq_send.at[i - 1], gq_recv.at[i - 1], (me, peer(i)))

    def query_send(i, carried):
        gq_out[i - 1] = query_part(peer(i)).astype(jnp.bfloat16)
        gq_copy(i).start()
        return carried

    query_send(1, 0)
    lax.fori_loop(1, min(2, chips - 1), ring_next, 0)
    lax.fori_loop(2, groups, query_send, 0)
    lax.fori_loop(2, chips - 1, ring_next, 0)
    gq_ref[...] = query_part(t)

    def unnormalized(grad, unit, inverse):
        grad = grad * SCALE
        return (grad - unit * jnp.sum(unit * grad, axis=1, keepdims=True)) * inverse

    value = gq_ref[...]
    for i in range(1, groups):
        gq_copy(i).wait_recv()
        value = value + gq_in[i - 1].astype(jnp.float32)
    own_rows = pl.ds(pl.multiple_of(t * part, part), part)
    blocks = [qraw[s, own_rows].astype(jnp.float32) for s in range(groups)]
    inverse = inverse_magnitude(blocks)
    gq_ref[...] = unnormalized(value, jnp.concatenate(blocks, axis=1) * inverse, inverse)

    value = key_part(me)
    sb_copy(chips - 1).wait_recv()
    value = value + sib_in[chips - 1].astype(jnp.float32)
    for h in range(HALVES):
        rg_copy(chips - 2, h).wait_recv()
    value = value + ring_in[chips - 2].astype(jnp.float32)
    blocks = [kraw[s].astype(jnp.float32) for s in range(groups)]
    inverse = inverse_magnitude(blocks)
    gk_ref[...] = unnormalized(value, jnp.concatenate(blocks, axis=1) * inverse, inverse)

    for i in range(1, groups):
        kx_copy(i).wait_send()
        qx_copy(i).wait_send()
        st_copy(i).wait_send()
        gq_copy(i).wait_send()
    for s in range(chips):
        sb_copy(s).wait_send()
        for h in range(HALVES):
            fwd_copy(s, h).wait_send()
            if s < chips - 1:
                ring_copy(s, h).wait_send()
                rg_copy(s, h).wait_send()


PIECES = 4


def deliver(
    loss_in, gq_in, gk_in, loss_out, gq_out, gk_out, loss_held, held, in_sems, out_sems, loss_sems
):
    part = gq_out.shape[0]
    start = pl.multiple_of(lax.axis_index("tensor") * part, part)
    copies = []
    for a, (src, dst) in enumerate(((gq_in, gq_out), (gk_in, gk_out))):
        for p in range(PIECES):
            span = pl.ds(p * (part // PIECES), part // PIECES)
            slot = held.at[a, span]
            copies.append((
                pltpu.make_async_copy(src.at[span], slot, in_sems.at[a, p]),
                pltpu.make_async_copy(slot, dst.at[span], out_sems.at[a, p]),
            ))
    copies.append((
        pltpu.make_async_copy(loss_in.at[:, pl.ds(start, part)], loss_held, loss_sems.at[0]),
        pltpu.make_async_copy(loss_held, loss_out, loss_sems.at[1]),
    ))
    for arrive, _ in copies:
        arrive.start()
    for arrive, leave in copies:
        arrive.wait()
        leave.start()
    for _, leave in copies:
        leave.wait()


def body(queries, keys, projection, positives):
    dp, groups = lax.axis_size("dp"), lax.axis_size("tensor")
    chips = dp // 2
    rows = queries.shape[0]
    part = rows // groups
    feats = projection.shape[1]
    width = feats * groups
    embed = queries.shape[1]
    slots = min(STAGE_BYTES // (rows * DEPTH * 2), embed // DEPTH)
    bf16, f32 = jnp.bfloat16, jnp.float32
    vmem, dma = pltpu.VMEM, pltpu.SemaphoreType.DMA
    spec = pl.BlockSpec(memory_space=pltpu.VMEM)
    loss, grad_q, grad_k = pl.pallas_call(
        functools.partial(kernel, chips, groups),
        out_shape=(
            jax.ShapeDtypeStruct((1, rows), f32),
            jax.ShapeDtypeStruct((part, width), f32),
            jax.ShapeDtypeStruct((part, width), f32),
        ),
        in_specs=[pl.BlockSpec(memory_space=pl.ANY)] * 3 + [spec],
        out_specs=(spec,) * 3,
        scratch_shapes=[
            vmem((slots, rows, DEPTH), bf16),
            vmem((embed, feats), bf16),
            vmem((rows, feats), bf16),
            vmem((groups, part, feats), bf16),
            vmem((dp, part, width), bf16),
            vmem((groups, rows, feats), bf16),
            vmem((rows, width), bf16),
            vmem((dp, part, rows), f32),
            vmem((dp, part, rows), bf16),
            vmem((groups, 8, rows), f32),
            vmem((chips, part, width), bf16),
            vmem((chips, part, width), bf16),
            vmem((chips - 1, part, width), bf16),
            vmem((groups - 1, part, width), bf16),
            vmem((groups - 1, part, width), bf16),
            dma((slots,)), dma((embed // DEPTH,)),
            dma((groups,)), dma((groups,)), dma((groups,)), dma((groups,)),
            dma((chips, HALVES)), dma((chips, HALVES)), dma((dp, HALVES)),
            dma((groups,)), dma((groups,)),
            dma((chips,)), dma((chips,)),
            dma((chips, HALVES)), dma((chips, HALVES)),
            dma((groups,)), dma((groups,)),
        ],
        compiler_params=pltpu.CompilerParams(
            collective_id=0, has_side_effects=True, vmem_limit_bytes=62 * 1024 * 1024
        ),
        cost_estimate=pl.CostEstimate(
            flops=8 * rows * dp * part * width + 4 * rows * embed * feats,
            bytes_accessed=(4 * rows + 2 * feats) * embed + 8 * part * width,
            transcendentals=2 * rows * dp * part,
        ),
    )(queries, keys, projection, positives)
    whole = pl.BlockSpec(memory_space=pl.ANY)
    pair_loss, grad_q, grad_k = pl.pallas_call(
        deliver,
        out_shape=(
            jax.ShapeDtypeStruct((1, part), f32),
            jax.ShapeDtypeStruct((part, width), f32),
            jax.ShapeDtypeStruct((part, width), f32),
        ),
        in_specs=[whole] * 3,
        out_specs=(whole,) * 3,
        scratch_shapes=[
            vmem((1, part), f32), vmem((2, part, width), f32),
            dma((2, PIECES)), dma((2, PIECES)), dma((2,)),
        ],
        compiler_params=pltpu.CompilerParams(vmem_limit_bytes=62 * 1024 * 1024),
        cost_estimate=pl.CostEstimate(
            flops=0, bytes_accessed=16 * part * width, transcendentals=0
        ),
    )(loss, grad_q, grad_k)
    return (pair_loss.reshape(part), grad_q, grad_k)


def solution(mesh):
    in_specs = (P("dp", None), P("dp", None), P(None, "tensor"), P("dp", None))
    out_specs = (P(("dp", "tensor")), P(("dp", "tensor"), None), P(("dp", "tensor"), None))
    return jax.shard_map(body, mesh=mesh, in_specs=in_specs, out_specs=out_specs, check_vma=False)
```

```python
import functools

import jax
import jax.numpy as jnp
from jax import lax
from jax.experimental import pallas as pl
from jax.experimental.pallas import tpu as pltpu
from jax.sharding import PartitionSpec as P

SCALE = 100.0
EPSILON = 1e-06
MESH = pl.DeviceIdType.MESH
SPLITS = 4
DEPTH = 512
STAGE_BYTES = 4 * 1024 * 1024


def kernel(
    chips, groups, q_hbm, k_hbm, w_hbm, pos_ref, loss_ref, gq_ref, gk_ref,
    stage, w_in, kfeat, kraw, kall, qraw, qhat, scores, weights, stats,
    sib_out, sib_in, ring_in, gq_out, gq_in, stage_sem, w_sem,
    kx_send, kx_recv, qx_send, qx_recv, ring_send, fwd_send, k_recv,
    st_send, st_recv, sb_send, sb_recv, rg_send, rg_recv, gq_send, gq_recv,
):
    rows, feats = kfeat.shape
    slots, steps = stage.shape[0], w_in.shape[0] // DEPTH
    part = rows // groups
    piece = part // SPLITS
    me = lax.axis_index("dp")
    t = lax.axis_index("tensor")
    chip, core = me // 2, me % 2
    other = 1 - core
    sibling = chip * 2 + other
    right = lax.rem(chip + 1, chips) * 2 + core
    left = lax.rem(chip + chips - 1, chips) * 2 + core

    def peer(i):
        return lax.rem(t + i, groups)

    def remote(src, dst, send, recv, device):
        return pltpu.make_async_remote_copy(
            src_ref=src, dst_ref=dst, send_sem=send, recv_sem=recv,
            device_id=device, device_id_type=MESH,
        )

    barrier = pltpu.get_barrier_semaphore()
    for i in range(1, groups):
        pl.semaphore_signal(barrier, inc=1, device_id=(me, peer(i)), device_id_type=MESH)
    for device in (sibling, right, left):
        pl.semaphore_signal(barrier, inc=1, device_id=(device, t), device_id_type=MESH)

    def w_copy(c):
        span = pl.ds(c * DEPTH, DEPTH)
        return pltpu.make_async_copy(w_hbm.at[span], w_in.at[span], w_sem.at[c])

    def stage_copy(c):
        source_ref = k_hbm if c < steps else q_hbm
        span = pl.ds((c % steps) * DEPTH, DEPTH)
        return pltpu.make_async_copy(
            source_ref.at[:, span], stage.at[c % slots], stage_sem.at[c % slots]
        )

    for c in range(max(steps, slots)):
        if c < steps:
            w_copy(c).start()
        if c < slots:
            stage_copy(c).start()

    def project(first):
        total = None
        for c in range(steps):
            if first == 0:
                w_copy(c).wait()
            stage_copy(first + c).wait()
            term = jnp.dot(
                stage[(first + c) % slots], w_in[c * DEPTH : (c + 1) * DEPTH],
                preferred_element_type=jnp.float32,
            )
            total = term if total is None else total + term
            if first + c + slots < 2 * steps:
                stage_copy(first + c + slots).start()
        return total.astype(jnp.bfloat16)

    kfeat[...] = project(0)
    pl.semaphore_wait(barrier, groups + 2)

    def kx_copy(i):
        rows_of = pl.ds(pl.multiple_of(peer(i) * part, part), part)
        return remote(kfeat.at[rows_of], kraw.at[t], kx_send.at[i], kx_recv.at[t], (me, peer(i)))

    def kx_from(i):
        slot = kraw.at[peer(i)]
        return remote(slot, slot, kx_send.at[i], kx_recv.at[peer(i)], (me, peer(i)))

    def qx_copy(i):
        return remote(qraw.at[t], qraw.at[t], qx_send.at[i], qx_recv.at[t], (me, peer(i)))

    def qx_from(i):
        slot = qraw.at[peer(i)]
        return remote(slot, slot, qx_send.at[i], qx_recv.at[peer(i)], (me, peer(i)))

    for i in range(1, groups):
        kx_copy(i).start()
    kraw[t] = kfeat[pl.ds(pl.multiple_of(t * part, part), part)]
    qraw[t] = project(steps)
    for i in range(1, groups):
        kx_from(i).wait_recv()

    def inverse_magnitude(blocks):
        total = blocks[0] * blocks[0]
        for block in blocks[1:]:
            total = total + block * block
        return lax.rsqrt(jnp.sum(total, axis=1, keepdims=True) + EPSILON)

    entries = [kraw[s].astype(jnp.float32) for s in range(groups)]
    k_inverse = inverse_magnitude(entries)
    for s in range(groups):
        kall[me, :, s * feats : (s + 1) * feats] = (entries[s] * k_inverse).astype(
            jnp.bfloat16
        )

    def source(s):
        return lax.rem(chip + chips - s, chips) * 2

    def ring_copy(s, h):
        slot = kall.at[source(s) + core, pl.ds(h * piece, piece)]
        return remote(slot, slot, ring_send.at[s, h], k_recv.at[source(s) + core, h], (right, t))

    def fwd_copy(s, h):
        slot = kall.at[source(s) + core, pl.ds(h * piece, piece)]
        return remote(slot, slot, fwd_send.at[s, h], k_recv.at[source(s) + core, h], (sibling, t))

    def k_from(index, h):
        slot = kall.at[index, pl.ds(h * piece, piece)]
        return remote(slot, slot, ring_send.at[0, h], k_recv.at[index, h], (right, t))

    def forward(s):
        for h in range(SPLITS):
            if s > 0:
                k_from(source(s) + core, h).wait_recv()
            if s < chips - 1:
                ring_copy(s, h).start()
            fwd_copy(s, h).start()

    forward(0)
    for i in range(1, groups):
        qx_copy(i).start()
    for s in range(1, chips - 1):
        forward(s)

    for i in range(1, groups):
        qx_from(i).wait_recv()

    def normalize_rows(p, carried):
        span = pl.ds(pl.multiple_of(p * part, part), part)
        blocks = [qraw[s, span].astype(jnp.float32) for s in range(groups)]
        inverse = inverse_magnitude(blocks)
        for s in range(groups):
            qhat[span, s * feats : (s + 1) * feats] = (blocks[s] * inverse).astype(jnp.bfloat16)
        return carried

    lax.fori_loop(0, groups, normalize_rows, 0)

    def score(index):
        block = SCALE * lax.dot_general(
            kall[index], qhat[...], (((1,), (1,)), ((), ())), preferred_element_type=jnp.float32
        )
        scores[index] = block
        return block

    def fold(index, state):
        row_max, row_sum = state
        block = score(index)
        new_max = jnp.maximum(row_max, jnp.max(block, axis=0, keepdims=True))
        row_sum = row_sum * jnp.exp(row_max - new_max) + jnp.sum(
            jnp.exp(block - new_max), axis=0, keepdims=True
        )
        return (new_max, row_sum)

    def positive_mask():
        key_index = lax.broadcasted_iota(jnp.int32, (part, rows), 0)
        return (key_index == pos_ref[...] - t * part).astype(jnp.float32)

    own = score(me)
    row_max = jnp.max(own, axis=0, keepdims=True)
    row_sum = jnp.sum(jnp.exp(own - row_max), axis=0, keepdims=True)
    matched = jnp.sum(own * positive_mask(), axis=0, keepdims=True)

    def from_sibling(s):
        for h in range(SPLITS):
            k_from(source(s) + other, h).wait_recv()

    def fold_pair(s, state):
        state = fold(source(s) + core, state)
        from_sibling(s)
        return fold(source(s) + other, state)

    from_sibling(0)
    state = fold(source(0) + other, (row_max, row_sum))
    state = lax.fori_loop(1, chips - 1, fold_pair, state)
    forward(chips - 1)
    row_max, row_sum = fold_pair(chips - 1, state)

    stats[t, 0:1] = row_max
    stats[t, 1:2] = row_sum
    stats[t, 2:3] = matched

    def st_copy(i):
        return remote(stats.at[t], stats.at[t], st_send.at[i], st_recv.at[t], (me, peer(i)))

    def st_from(i):
        slot = stats.at[peer(i)]
        return remote(slot, slot, st_send.at[i], st_recv.at[peer(i)], (me, peer(i)))

    for i in range(1, groups):
        st_copy(i).start()
    for i in range(1, groups):
        st_from(i).wait_recv()
    best = stats[0, 0:1]
    for s in range(1, groups):
        best = jnp.maximum(best, stats[s, 0:1])
    total = jnp.zeros_like(best)
    matched = jnp.zeros_like(best)
    for s in range(groups):
        total = total + stats[s, 1:2] * jnp.exp(stats[s, 0:1] - best)
        matched = matched + stats[s, 2:3]
    log_total = best + jnp.log(total)
    loss_ref[...] = log_total - matched

    def weigh(index, carried):
        weights[index] = jnp.exp(scores[index] - log_total).astype(jnp.bfloat16)
        return carried

    def target(i):
        return lax.rem(chip + 2 * chips - 1 - i, chips) * 2

    def key_part(index):
        return jnp.dot(weights[index], qhat[...], preferred_element_type=jnp.float32)

    def sb_copy(i):
        return remote(sib_out.at[i], sib_in.at[i], sb_send.at[i], sb_recv.at[i], (sibling, t))

    def rg_copy(i, h):
        span = pl.ds(h * piece, piece)
        return remote(
            sib_in.at[i, span], ring_in.at[i, span], rg_send.at[i, h], rg_recv.at[i, h], (right, t)
        )

    def hand_over(i, carried):
        sib_out[i] = key_part(target(i) + other).astype(jnp.bfloat16)
        sb_copy(i).start()
        return carried

    def ring_first():
        value = key_part(target(0) + core)
        sb_copy(0).wait_recv()
        for h in range(SPLITS):
            span = slice(h * piece, (h + 1) * piece)
            sib_in[0, span] = (value[span] + sib_in[0, span].astype(jnp.float32)).astype(jnp.bfloat16)
            rg_copy(0, h).start()

    def ring_next(i, carried):
        value = key_part(target(i) + core)
        sb_copy(i).wait_recv()
        for h in range(SPLITS):
            span = slice(h * piece, (h + 1) * piece)
            both = value[span] + sib_in[i, span].astype(jnp.float32)
            rg_copy(i - 1, h).wait_recv()
            sib_in[i, span] = (both + ring_in[i - 1, span].astype(jnp.float32)).astype(jnp.bfloat16)
            rg_copy(i, h).start()
        return carried

    def weigh_pair(i, carried):
        weigh(target(i) + other, 0)
        hand_over(i, 0)
        return weigh(target(i) + core, carried)

    weigh_pair(0, 0)
    ring_first()
    lax.fori_loop(1, chips - 1, weigh_pair, 0)
    weigh(sibling, 0)
    hand_over(chips - 1, 0)
    weights[me] = (jnp.exp(scores[me] - log_total) - positive_mask()).astype(jnp.bfloat16)

    def query_part(p):
        span = pl.ds(pl.multiple_of(p * part, part), part)
        chosen = weights[:, :, span].reshape(2 * chips * part, part)
        keys = kall[...].reshape(2 * chips * part, groups * feats)
        return lax.dot_general(
            chosen, keys, (((0,), (0,)), ((), ())), preferred_element_type=jnp.float32
        )

    def gq_copy(i):
        return remote(gq_out.at[i - 1], gq_in.at[i - 1], gq_send.at[i - 1], gq_recv.at[i - 1], (me, peer(i)))

    def query_send(i, carried):
        gq_out[i - 1] = query_part(peer(i)).astype(jnp.bfloat16)
        gq_copy(i).start()
        return carried

    query_send(1, 0)
    lax.fori_loop(1, min(2, chips - 1), ring_next, 0)
    lax.fori_loop(2, groups, query_send, 0)
    lax.fori_loop(2, chips - 1, ring_next, 0)
    gq_ref[...] = query_part(t)

    def unnormalized(grad, unit, inverse):
        grad = grad * SCALE
        return (grad - unit * jnp.sum(unit * grad, axis=1, keepdims=True)) * inverse

    value = gq_ref[...]
    for i in range(1, groups):
        gq_copy(i).wait_recv()
        value = value + gq_in[i - 1].astype(jnp.float32)
    own_rows = pl.ds(pl.multiple_of(t * part, part), part)
    blocks = [qraw[s, own_rows].astype(jnp.float32) for s in range(groups)]
    inverse = inverse_magnitude(blocks)
    gq_ref[...] = unnormalized(value, jnp.concatenate(blocks, axis=1) * inverse, inverse)

    value = key_part(me)
    sb_copy(chips - 1).wait_recv()
    value = value + sib_in[chips - 1].astype(jnp.float32)
    for h in range(SPLITS):
        rg_copy(chips - 2, h).wait_recv()
    value = value + ring_in[chips - 2].astype(jnp.float32)
    blocks = [kraw[s].astype(jnp.float32) for s in range(groups)]
    inverse = inverse_magnitude(blocks)
    gk_ref[...] = unnormalized(value, jnp.concatenate(blocks, axis=1) * inverse, inverse)

    for i in range(1, groups):
        kx_copy(i).wait_send()
        qx_copy(i).wait_send()
        st_copy(i).wait_send()
        gq_copy(i).wait_send()
    for s in range(chips):
        sb_copy(s).wait_send()
        for h in range(SPLITS):
            fwd_copy(s, h).wait_send()
            if s < chips - 1:
                ring_copy(s, h).wait_send()
                rg_copy(s, h).wait_send()


PIECES = 4


def deliver(
    loss_in, gq_in, gk_in, loss_out, gq_out, gk_out, loss_held, held, in_sems, out_sems, loss_sems
):
    part = gq_out.shape[0]
    start = pl.multiple_of(lax.axis_index("tensor") * part, part)
    copies = []
    for a, (src, dst) in enumerate(((gq_in, gq_out), (gk_in, gk_out))):
        for p in range(PIECES):
            span = pl.ds(p * (part // PIECES), part // PIECES)
            slot = held.at[a, span]
            copies.append((
                pltpu.make_async_copy(src.at[span], slot, in_sems.at[a, p]),
                pltpu.make_async_copy(slot, dst.at[span], out_sems.at[a, p]),
            ))
    copies.append((
        pltpu.make_async_copy(loss_in.at[:, pl.ds(start, part)], loss_held, loss_sems.at[0]),
        pltpu.make_async_copy(loss_held, loss_out, loss_sems.at[1]),
    ))
    for arrive, _ in copies:
        arrive.start()
    for arrive, leave in copies:
        arrive.wait()
        leave.start()
    for _, leave in copies:
        leave.wait()


def body(queries, keys, projection, positives):
    dp, groups = lax.axis_size("dp"), lax.axis_size("tensor")
    chips = dp // 2
    rows = queries.shape[0]
    part = rows // groups
    feats = projection.shape[1]
    width = feats * groups
    embed = queries.shape[1]
    slots = min(STAGE_BYTES // (rows * DEPTH * 2), embed // DEPTH)
    bf16, f32 = jnp.bfloat16, jnp.float32
    vmem, dma = pltpu.VMEM, pltpu.SemaphoreType.DMA
    spec = pl.BlockSpec(memory_space=pltpu.VMEM)
    loss, grad_q, grad_k = pl.pallas_call(
        functools.partial(kernel, chips, groups),
        out_shape=(
            jax.ShapeDtypeStruct((1, rows), f32),
            jax.ShapeDtypeStruct((part, width), f32),
            jax.ShapeDtypeStruct((part, width), f32),
        ),
        in_specs=[pl.BlockSpec(memory_space=pl.ANY)] * 3 + [spec],
        out_specs=(spec,) * 3,
        scratch_shapes=[
            vmem((slots, rows, DEPTH), bf16),
            vmem((embed, feats), bf16),
            vmem((rows, feats), bf16),
            vmem((groups, part, feats), bf16),
            vmem((dp, part, width), bf16),
            vmem((groups, rows, feats), bf16),
            vmem((rows, width), bf16),
            vmem((dp, part, rows), f32),
            vmem((dp, part, rows), bf16),
            vmem((groups, 8, rows), f32),
            vmem((chips, part, width), bf16),
            vmem((chips, part, width), bf16),
            vmem((chips - 1, part, width), bf16),
            vmem((groups - 1, part, width), bf16),
            vmem((groups - 1, part, width), bf16),
            dma((slots,)), dma((embed // DEPTH,)),
            dma((groups,)), dma((groups,)), dma((groups,)), dma((groups,)),
            dma((chips, SPLITS)), dma((chips, SPLITS)), dma((dp, SPLITS)),
            dma((groups,)), dma((groups,)),
            dma((chips,)), dma((chips,)),
            dma((chips, SPLITS)), dma((chips, SPLITS)),
            dma((groups,)), dma((groups,)),
        ],
        compiler_params=pltpu.CompilerParams(
            collective_id=0, has_side_effects=True, vmem_limit_bytes=62 * 1024 * 1024
        ),
        cost_estimate=pl.CostEstimate(
            flops=8 * rows * dp * part * width + 4 * rows * embed * feats,
            bytes_accessed=(4 * rows + 2 * feats) * embed + 8 * part * width,
            transcendentals=2 * rows * dp * part,
        ),
    )(queries, keys, projection, positives)
    whole = pl.BlockSpec(memory_space=pl.ANY)
    pair_loss, grad_q, grad_k = pl.pallas_call(
        deliver,
        out_shape=(
            jax.ShapeDtypeStruct((1, part), f32),
            jax.ShapeDtypeStruct((part, width), f32),
            jax.ShapeDtypeStruct((part, width), f32),
        ),
        in_specs=[whole] * 3,
        out_specs=(whole,) * 3,
        scratch_shapes=[
            vmem((1, part), f32), vmem((2, part, width), f32),
            dma((2, PIECES)), dma((2, PIECES)), dma((2,)),
        ],
        compiler_params=pltpu.CompilerParams(vmem_limit_bytes=62 * 1024 * 1024),
        cost_estimate=pl.CostEstimate(
            flops=0, bytes_accessed=16 * part * width, transcendentals=0
        ),
    )(loss, grad_q, grad_k)
    return (pair_loss.reshape(part), grad_q, grad_k)


def solution(mesh):
    in_specs = (P("dp", None), P("dp", None), P(None, "tensor"), P("dp", None))
    out_specs = (P(("dp", "tensor")), P(("dp", "tensor"), None), P(("dp", "tensor"), None))
    return jax.shard_map(body, mesh=mesh, in_specs=in_specs, out_specs=out_specs, check_vma=False)
```

```python
import functools

import jax
import jax.numpy as jnp
from jax import lax
from jax.experimental import pallas as pl
from jax.experimental.pallas import tpu as pltpu
from jax.sharding import PartitionSpec as P

SCALE = 100.0
EPSILON = 1e-06
MESH = pl.DeviceIdType.MESH
HALVES = 2
DEPTH = 512
STAGE_BYTES = 4 * 1024 * 1024


def kernel(
    chips, groups, q_hbm, k_hbm, w_hbm, pos_ref, loss_ref, gq_ref, gk_ref,
    stage, w_in, kfeat, kraw, kall, qraw, qhat, scores, weights, stats,
    sib_out, sib_in, ring_in, gq_out, gq_in, stage_sem, w_sem,
    kx_send, kx_recv, qx_send, qx_recv, ring_send, fwd_send, k_recv,
    st_send, st_recv, sb_send, sb_recv, rg_send, rg_recv, gq_send, gq_recv,
):
    rows, feats = kfeat.shape
    slots, steps = stage.shape[0], w_in.shape[0] // DEPTH
    part = rows // groups
    half = part // HALVES
    me = lax.axis_index("dp")
    t = lax.axis_index("tensor")
    chip, core = me // 2, me % 2
    other = 1 - core
    sibling = chip * 2 + other
    right = lax.rem(chip + 1, chips) * 2 + core
    left = lax.rem(chip + chips - 1, chips) * 2 + core

    def peer(i):
        return lax.rem(t + i, groups)

    def remote(src, dst, send, recv, device):
        return pltpu.make_async_remote_copy(
            src_ref=src, dst_ref=dst, send_sem=send, recv_sem=recv,
            device_id=device, device_id_type=MESH,
        )

    barrier = pltpu.get_barrier_semaphore()
    for i in range(1, groups):
        pl.semaphore_signal(barrier, inc=1, device_id=(me, peer(i)), device_id_type=MESH)
    for device in (sibling, right, left):
        pl.semaphore_signal(barrier, inc=1, device_id=(device, t), device_id_type=MESH)

    def w_copy(c):
        span = pl.ds(c * DEPTH, DEPTH)
        return pltpu.make_async_copy(w_hbm.at[span], w_in.at[span], w_sem.at[c])

    def stage_copy(c):
        source_ref = k_hbm if c < steps else q_hbm
        span = pl.ds((c % steps) * DEPTH, DEPTH)
        return pltpu.make_async_copy(
            source_ref.at[:, span], stage.at[c % slots], stage_sem.at[c % slots]
        )

    for c in range(max(steps, slots)):
        if c < steps:
            w_copy(c).start()
        if c < slots:
            stage_copy(c).start()

    def project(first):
        total = None
        for c in range(steps):
            if first == 0:
                w_copy(c).wait()
            stage_copy(first + c).wait()
            term = jnp.dot(
                stage[(first + c) % slots], w_in[c * DEPTH : (c + 1) * DEPTH],
                preferred_element_type=jnp.float32,
            )
            total = term if total is None else total + term
            if first + c + slots < 2 * steps:
                stage_copy(first + c + slots).start()
        return total.astype(jnp.bfloat16)

    kfeat[...] = project(0)
    pl.semaphore_wait(barrier, groups + 2)

    def kx_copy(i):
        rows_of = pl.ds(pl.multiple_of(peer(i) * part, part), part)
        return remote(kfeat.at[rows_of], kraw.at[t], kx_send.at[i], kx_recv.at[t], (me, peer(i)))

    def kx_from(i):
        slot = kraw.at[peer(i)]
        return remote(slot, slot, kx_send.at[i], kx_recv.at[peer(i)], (me, peer(i)))

    def qx_copy(i):
        return remote(qraw.at[t], qraw.at[t], qx_send.at[i], qx_recv.at[t], (me, peer(i)))

    def qx_from(i):
        slot = qraw.at[peer(i)]
        return remote(slot, slot, qx_send.at[i], qx_recv.at[peer(i)], (me, peer(i)))

    for i in range(1, groups):
        kx_copy(i).start()
    kraw[t] = kfeat[pl.ds(pl.multiple_of(t * part, part), part)]
    qraw[t] = project(steps)
    for i in range(1, groups):
        kx_from(i).wait_recv()

    def inverse_magnitude(blocks):
        total = blocks[0] * blocks[0]
        for block in blocks[1:]:
            total = total + block * block
        return lax.rsqrt(jnp.sum(total, axis=1, keepdims=True) + EPSILON)

    entries = [kraw[s].astype(jnp.float32) for s in range(groups)]
    k_inverse = inverse_magnitude(entries)
    for s in range(groups):
        kall[me, :, s * feats : (s + 1) * feats] = (entries[s] * k_inverse).astype(
            jnp.bfloat16
        )

    def source(s):
        return lax.rem(chip + chips - s, chips) * 2

    def ring_copy(s, h):
        slot = kall.at[source(s) + core, pl.ds(h * half, half)]
        return remote(slot, slot, ring_send.at[s, h], k_recv.at[source(s) + core, h], (right, t))

    def fwd_copy(s, h):
        slot = kall.at[source(s) + core, pl.ds(h * half, half)]
        return remote(slot, slot, fwd_send.at[s, h], k_recv.at[source(s) + core, h], (sibling, t))

    def k_from(index, h):
        slot = kall.at[index, pl.ds(h * half, half)]
        return remote(slot, slot, ring_send.at[0, h], k_recv.at[index, h], (right, t))

    def forward(s):
        for h in range(HALVES):
            if s > 0:
                k_from(source(s) + core, h).wait_recv()
            if s < chips - 1:
                ring_copy(s, h).start()
            fwd_copy(s, h).start()

    forward(0)
    for i in range(1, groups):
        qx_copy(i).start()
    for s in range(1, chips - 1):
        forward(s)

    for i in range(1, groups):
        qx_from(i).wait_recv()

    def normalize_rows(p, carried):
        span = pl.ds(pl.multiple_of(p * part, part), part)
        blocks = [qraw[s, span].astype(jnp.float32) for s in range(groups)]
        inverse = inverse_magnitude(blocks)
        for s in range(groups):
            qhat[span, s * feats : (s + 1) * feats] = (blocks[s] * inverse).astype(jnp.bfloat16)
        return carried

    lax.fori_loop(0, groups, normalize_rows, 0)

    def score(index):
        block = SCALE * lax.dot_general(
            kall[index], qhat[...], (((1,), (1,)), ((), ())), preferred_element_type=jnp.float32
        )
        scores[index] = block
        return block

    def fold(index, state):
        row_max, row_sum = state
        block = score(index)
        new_max = jnp.maximum(row_max, jnp.max(block, axis=0, keepdims=True))
        row_sum = row_sum * jnp.exp(row_max - new_max) + jnp.sum(
            jnp.exp(block - new_max), axis=0, keepdims=True
        )
        return (new_max, row_sum)

    def positive_mask():
        key_index = lax.broadcasted_iota(jnp.int32, (part, rows), 0)
        return (key_index == pos_ref[...] - t * part).astype(jnp.float32)

    own = score(me)
    row_max = jnp.max(own, axis=0, keepdims=True)
    row_sum = jnp.sum(jnp.exp(own - row_max), axis=0, keepdims=True)
    matched = jnp.sum(own * positive_mask(), axis=0, keepdims=True)

    def from_sibling(s):
        for h in range(HALVES):
            k_from(source(s) + other, h).wait_recv()

    def fold_pair(s, state):
        state = fold(source(s) + core, state)
        from_sibling(s)
        return fold(source(s) + other, state)

    from_sibling(0)
    state = fold(source(0) + other, (row_max, row_sum))
    state = lax.fori_loop(1, chips - 1, fold_pair, state)
    forward(chips - 1)
    row_max, row_sum = fold_pair(chips - 1, state)

    stats[t, 0:1] = row_max
    stats[t, 1:2] = row_sum
    stats[t, 2:3] = matched

    def st_copy(i):
        return remote(stats.at[t], stats.at[t], st_send.at[i], st_recv.at[t], (me, peer(i)))

    def st_from(i):
        slot = stats.at[peer(i)]
        return remote(slot, slot, st_send.at[i], st_recv.at[peer(i)], (me, peer(i)))

    for i in range(1, groups):
        st_copy(i).start()
    for i in range(1, groups):
        st_from(i).wait_recv()
    best = stats[0, 0:1]
    for s in range(1, groups):
        best = jnp.maximum(best, stats[s, 0:1])
    total = jnp.zeros_like(best)
    matched = jnp.zeros_like(best)
    for s in range(groups):
        total = total + stats[s, 1:2] * jnp.exp(stats[s, 0:1] - best)
        matched = matched + stats[s, 2:3]
    log_total = best + jnp.log(total)
    loss_ref[...] = log_total - matched

    def weigh(index, carried):
        weights[index] = jnp.exp(scores[index] - log_total).astype(jnp.bfloat16)
        return carried

    def target(i):
        return lax.rem(chip + 2 * chips - 1 - i, chips) * 2

    def key_part(index):
        return jnp.dot(weights[index], qhat[...], preferred_element_type=jnp.float32)

    def sb_copy(i):
        return remote(sib_out.at[i], sib_in.at[i], sb_send.at[i], sb_recv.at[i], (sibling, t))

    def rg_copy(i, h):
        span = pl.ds(h * half, half)
        return remote(
            sib_in.at[i, span], ring_in.at[i, span], rg_send.at[i, h], rg_recv.at[i, h], (right, t)
        )

    def hand_over(i, carried):
        sib_out[i] = key_part(target(i) + other).astype(jnp.bfloat16)
        sb_copy(i).start()
        return carried

    def ring_first():
        value = key_part(target(0) + core)
        sb_copy(0).wait_recv()
        for h in range(HALVES):
            span = slice(h * half, (h + 1) * half)
            sib_in[0, span] = (value[span] + sib_in[0, span].astype(jnp.float32)).astype(jnp.bfloat16)
            rg_copy(0, h).start()

    def ring_next(i, carried):
        value = key_part(target(i) + core)
        sb_copy(i).wait_recv()
        for h in range(HALVES):
            span = slice(h * half, (h + 1) * half)
            both = value[span] + sib_in[i, span].astype(jnp.float32)
            rg_copy(i - 1, h).wait_recv()
            sib_in[i, span] = (both + ring_in[i - 1, span].astype(jnp.float32)).astype(jnp.bfloat16)
            rg_copy(i, h).start()
        return carried

    def weigh_pair(i, carried):
        weigh(target(i) + other, 0)
        hand_over(i, 0)
        return weigh(target(i) + core, carried)

    weigh_pair(0, 0)
    ring_first()
    lax.fori_loop(1, chips - 1, weigh_pair, 0)
    weigh(sibling, 0)
    hand_over(chips - 1, 0)
    weights[me] = (jnp.exp(scores[me] - log_total) - positive_mask()).astype(jnp.bfloat16)

    def query_part(p):
        span = pl.ds(pl.multiple_of(p * part, part), part)
        chosen = weights[:, :, span].reshape(2 * chips * part, part)
        keys = kall[...].reshape(2 * chips * part, groups * feats)
        return lax.dot_general(
            chosen, keys, (((0,), (0,)), ((), ())), preferred_element_type=jnp.float32
        )

    def gq_copy(i):
        return remote(gq_out.at[i - 1], gq_in.at[i - 1], gq_send.at[i - 1], gq_recv.at[i - 1], (me, peer(i)))

    def query_send(i, carried):
        gq_out[i - 1] = query_part(peer(i)).astype(jnp.bfloat16)
        gq_copy(i).start()
        return carried

    lax.fori_loop(1, min(2, chips - 1), ring_next, 0)
    lax.fori_loop(1, groups, query_send, 0)
    lax.fori_loop(2, chips - 1, ring_next, 0)
    gq_ref[...] = query_part(t)

    def unnormalized(grad, unit, inverse):
        grad = grad * SCALE
        return (grad - unit * jnp.sum(unit * grad, axis=1, keepdims=True)) * inverse

    value = gq_ref[...]
    for i in range(1, groups):
        gq_copy(i).wait_recv()
        value = value + gq_in[i - 1].astype(jnp.float32)
    own_rows = pl.ds(pl.multiple_of(t * part, part), part)
    blocks = [qraw[s, own_rows].astype(jnp.float32) for s in range(groups)]
    inverse = inverse_magnitude(blocks)
    gq_ref[...] = unnormalized(value, jnp.concatenate(blocks, axis=1) * inverse, inverse)

    value = key_part(me)
    sb_copy(chips - 1).wait_recv()
    value = value + sib_in[chips - 1].astype(jnp.float32)
    for h in range(HALVES):
        rg_copy(chips - 2, h).wait_recv()
    value = value + ring_in[chips - 2].astype(jnp.float32)
    blocks = [kraw[s].astype(jnp.float32) for s in range(groups)]
    inverse = inverse_magnitude(blocks)
    gk_ref[...] = unnormalized(value, jnp.concatenate(blocks, axis=1) * inverse, inverse)

    for i in range(1, groups):
        kx_copy(i).wait_send()
        qx_copy(i).wait_send()
        st_copy(i).wait_send()
        gq_copy(i).wait_send()
    for s in range(chips):
        sb_copy(s).wait_send()
        for h in range(HALVES):
            fwd_copy(s, h).wait_send()
            if s < chips - 1:
                ring_copy(s, h).wait_send()
                rg_copy(s, h).wait_send()


PIECES = 4


def deliver(
    loss_in, gq_in, gk_in, loss_out, gq_out, gk_out, loss_held, held, in_sems, out_sems, loss_sems
):
    part = gq_out.shape[0]
    start = pl.multiple_of(lax.axis_index("tensor") * part, part)
    copies = []
    for a, (src, dst) in enumerate(((gq_in, gq_out), (gk_in, gk_out))):
        for p in range(PIECES):
            span = pl.ds(p * (part // PIECES), part // PIECES)
            slot = held.at[a, span]
            copies.append((
                pltpu.make_async_copy(src.at[span], slot, in_sems.at[a, p]),
                pltpu.make_async_copy(slot, dst.at[span], out_sems.at[a, p]),
            ))
    copies.append((
        pltpu.make_async_copy(loss_in.at[:, pl.ds(start, part)], loss_held, loss_sems.at[0]),
        pltpu.make_async_copy(loss_held, loss_out, loss_sems.at[1]),
    ))
    for arrive, _ in copies:
        arrive.start()
    for arrive, leave in copies:
        arrive.wait()
        leave.start()
    for _, leave in copies:
        leave.wait()


def body(queries, keys, projection, positives):
    dp, groups = lax.axis_size("dp"), lax.axis_size("tensor")
    chips = dp // 2
    rows = queries.shape[0]
    part = rows // groups
    feats = projection.shape[1]
    width = feats * groups
    embed = queries.shape[1]
    slots = min(STAGE_BYTES // (rows * DEPTH * 2), embed // DEPTH)
    bf16, f32 = jnp.bfloat16, jnp.float32
    vmem, dma = pltpu.VMEM, pltpu.SemaphoreType.DMA
    spec = pl.BlockSpec(memory_space=pltpu.VMEM)
    loss, grad_q, grad_k = pl.pallas_call(
        functools.partial(kernel, chips, groups),
        out_shape=(
            jax.ShapeDtypeStruct((1, rows), f32),
            jax.ShapeDtypeStruct((part, width), f32),
            jax.ShapeDtypeStruct((part, width), f32),
        ),
        in_specs=[pl.BlockSpec(memory_space=pl.ANY)] * 3 + [spec],
        out_specs=(spec,) * 3,
        scratch_shapes=[
            vmem((slots, rows, DEPTH), bf16),
            vmem((embed, feats), bf16),
            vmem((rows, feats), bf16),
            vmem((groups, part, feats), bf16),
            vmem((dp, part, width), bf16),
            vmem((groups, rows, feats), bf16),
            vmem((rows, width), bf16),
            vmem((dp, part, rows), f32),
            vmem((dp, part, rows), bf16),
            vmem((groups, 8, rows), f32),
            vmem((chips, part, width), bf16),
            vmem((chips, part, width), bf16),
            vmem((chips - 1, part, width), bf16),
            vmem((groups - 1, part, width), bf16),
            vmem((groups - 1, part, width), bf16),
            dma((slots,)), dma((embed // DEPTH,)),
            dma((groups,)), dma((groups,)), dma((groups,)), dma((groups,)),
            dma((chips, HALVES)), dma((chips, HALVES)), dma((dp, HALVES)),
            dma((groups,)), dma((groups,)),
            dma((chips,)), dma((chips,)),
            dma((chips, HALVES)), dma((chips, HALVES)),
            dma((groups,)), dma((groups,)),
        ],
        compiler_params=pltpu.CompilerParams(
            collective_id=0, has_side_effects=True, vmem_limit_bytes=62 * 1024 * 1024
        ),
        cost_estimate=pl.CostEstimate(
            flops=8 * rows * dp * part * width + 4 * rows * embed * feats,
            bytes_accessed=(4 * rows + 2 * feats) * embed + 8 * part * width,
            transcendentals=2 * rows * dp * part,
        ),
    )(queries, keys, projection, positives)
    whole = pl.BlockSpec(memory_space=pl.ANY)
    pair_loss, grad_q, grad_k = pl.pallas_call(
        deliver,
        out_shape=(
            jax.ShapeDtypeStruct((1, part), f32),
            jax.ShapeDtypeStruct((part, width), f32),
            jax.ShapeDtypeStruct((part, width), f32),
        ),
        in_specs=[whole] * 3,
        out_specs=(whole,) * 3,
        scratch_shapes=[
            vmem((1, part), f32), vmem((2, part, width), f32),
            dma((2, PIECES)), dma((2, PIECES)), dma((2,)),
        ],
        compiler_params=pltpu.CompilerParams(vmem_limit_bytes=62 * 1024 * 1024),
        cost_estimate=pl.CostEstimate(
            flops=0, bytes_accessed=16 * part * width, transcendentals=0
        ),
    )(loss, grad_q, grad_k)
    return (pair_loss.reshape(part), grad_q, grad_k)


def solution(mesh):
    in_specs = (P("dp", None), P("dp", None), P(None, "tensor"), P("dp", None))
    out_specs = (P(("dp", "tensor")), P(("dp", "tensor"), None), P(("dp", "tensor"), None))
    return jax.shard_map(body, mesh=mesh, in_specs=in_specs, out_specs=out_specs, check_vma=False)
```
